32 devices in a mesh: seq: 8 (over z, y), head: 4 (over x, core).
Axes of the slice: x: 2, y: 2, z: 4, core: 2. Of those that a mesh axis runs over, the one named last changes fastest.
Arguments:
- queries: bfloat16 [4096, 2048], P('seq', 'head'), may hold values from -5 to 5
- keys: bfloat16 [4096, 2048], P('seq', 'head'), may hold values from -5 to 5
- values: bfloat16 [4096, 2048], P('seq', 'head'), may hold values from -5 to 5
- out_weight: bfloat16 [2048, 2048], P('head'), may hold values from -0.125 to 0.125
- out_grad: bfloat16 [4096, 2048], P('seq'), may hold values from -5 to 5
- global_pos: int32 [256], replicated, may hold values from 0 to 511, as said below
- block_mask: int32 [32, 4], P('seq'), may hold values 0 or 1
Outputs:
- layer_out: bfloat16 [4096, 2048], P('seq', 'head')
- grad_queries: bfloat16 [4096, 2048], P('seq', 'head')
- grad_keys: bfloat16 [4096, 2048], P('seq', 'head')
- grad_values: bfloat16 [4096, 2048], P('seq', 'head')
The draws below stay inside these ranges and needn't reach their ends.
Inputs may be any that keep to these rules, and one draw needn't show every extreme that they name: `global_pos`: 256 distinct positions among the first 512 tokens.
All inputs are finite; a program needn't handle non-finite values. No bound on the sum of `block_mask` on one device may be relied on, other than what follows from the above.
Results may differ from the reference program's by a relative error of at most 0.012.
Values may be sent and summed in bfloat16 or wider, within the bound.
No kernel may reach another device: no remote copies, remote signals or barrier semaphores. Data moves between devices by JAX's collectives and lax.ppermute only.
A program may use at most 192 MiB of HBM per device.

```python
import math
import jax
import jax.numpy as jnp
from jax import lax

HEADS = 16
HEAD_DIM = 128
D = 2048
BLOCK = 128
WBLK = 4
GLOBALS = 256
TOK_DEV = 512
TOKENS = 4096
NBLK = 32


def draw_queries(key, part):
    own_key = jax.random.fold_in(key, 1)
    return jnp.clip(jax.random.normal(own_key, (TOKENS, D), jnp.float32), -4.0, 4.0).astype(jnp.bfloat16)


def draw_keys(key, part):
    own_key = jax.random.fold_in(key, 2)
    return jnp.clip(jax.random.normal(own_key, (TOKENS, D), jnp.float32), -4.0, 4.0).astype(jnp.bfloat16)


def draw_global_pos(key, part):
    inner = jax.random.permutation(key, TOK_DEV - 2)[:GLOBALS - 2].astype(jnp.int32) + 1
    both = jnp.concatenate([jnp.array([0, TOK_DEV - 1], jnp.int32), inner])
    order = jax.random.permutation(jax.random.fold_in(key, 3), GLOBALS)
    return both[order]


def with_ends(entries, rng, smallest, top_value):
    longest = entries.shape.index(max(entries.shape))
    spots = []
    for shift in (0, 1):
        where = [jax.random.randint(jax.random.fold_in(rng, axis), (), 0, length) for axis, length in enumerate(entries.shape)]
        where[longest] = (where[longest] + shift) % entries.shape[longest]
        spots.append(tuple(where))
    return entries.at[spots[0]].set(smallest).at[spots[1]].set(top_value)


def shard_levels(key, dims, split, low, high):
    loudness, own = 1.0, jax.random.fold_in(key, 6)
    for axis_at, parts in split:
        steps = jnp.exp(jax.random.uniform(jax.random.fold_in(own, axis_at), (parts,), jnp.float32, low / len(split), high / len(split)))
        loudness = loudness * jnp.repeat(steps, dims[axis_at] // parts).reshape([-1 if axis == axis_at else 1 for axis in range(len(dims))])
    return loudness


def gaussian(stream_key, shape, spread, reach, split=(), kind=jnp.bfloat16):
    drawn = jax.random.normal(stream_key, shape, jnp.float32) * spread
    if len(split) > 0:
        drawn = shard_levels(stream_key, shape, split, -0.22, 0.18) * drawn
    return jnp.clip(drawn, min=-reach, max=reach).astype(kind)


def setup_inputs(seed: int = 0) -> dict:
    seeds = jax.random.split(jax.random.key(seed), 8)
    queries = draw_queries(jax.random.fold_in(seeds[7], 71), 0)
    keys = draw_keys(jax.random.fold_in(seeds[7], 71), 0)
    values = gaussian(seeds[2], (TOKENS, D), 1.0, 5.0, ((0, 8), (1, 4)))
    out_weight = gaussian(seeds[3], (D, D), D ** -0.5, 0.125, ((0, 4),))
    out_grad = gaussian(seeds[4], (TOKENS, D), 1.0, 5.0, ((0, 8),))
    global_pos = draw_global_pos(jax.random.fold_in(seeds[7], 71), 0)
    block_mask = with_ends((jax.random.randint(seeds[6], (NBLK, WBLK), 0, 4) < 3).astype(jnp.int32), jax.random.fold_in(seeds[6], 1), 0, 1)
    return {"queries": queries, "keys": keys, "values": values, "out_weight": out_weight, "out_grad": out_grad, "global_pos": global_pos, "block_mask": block_mask}


def window_view(matrix):
    lead_rows = (WBLK - 1) * BLOCK
    padded = jnp.concatenate([jnp.zeros((lead_rows,) + matrix.shape[1:], matrix.dtype), matrix], axis=0)
    blocks = padded.reshape((NBLK + WBLK - 1, BLOCK) + matrix.shape[1:])
    return jnp.stack([blocks[WBLK - 1 - offset:WBLK - 1 - offset + NBLK] for offset in range(WBLK)], axis=1)

def window_fold(window_terms):
    summed = jnp.zeros((NBLK + WBLK - 1,) + window_terms.shape[2:], jnp.float32)
    for offset in range(WBLK):
        summed = summed.at[WBLK - 1 - offset:WBLK - 1 - offset + NBLK].add(window_terms[:, offset])
    return summed[WBLK - 1:].reshape((TOKENS,) + window_terms.shape[3:])

def rounded(values_f32):
    return lax.optimization_barrier(values_f32.astype(jnp.bfloat16)).astype(jnp.float32)

def reference(queries, keys, values, out_weight, out_grad, global_pos, block_mask):
    exact_prec = lax.Precision.HIGHEST
    score_scale = 1.0 / math.sqrt(HEAD_DIM)
    is_global = jnp.zeros((TOKENS,), jnp.int32).at[global_pos].set(1) > 0
    d_attn = jnp.dot(out_grad, out_weight.T, preferred_element_type=jnp.float32).astype(jnp.bfloat16)
    block_idx = jnp.arange(NBLK)[:, None, None, None]
    rel_block = jnp.arange(WBLK)[None, None, :, None]
    query_in = jnp.arange(BLOCK)[None, :, None, None]
    key_in = jnp.arange(BLOCK)[None, None, None, :]
    block_ok = block_mask[:, None, :, None] == 1
    key_global = window_view(is_global.astype(jnp.int32))[:, None, :, :] > 0
    pair_ok = (block_idx - rel_block >= 0) & block_ok & ((rel_block > 0) | (key_in <= query_in)) & jnp.logical_not(key_global)

    def one_head(operands):
        query_head, key_head, value_head, dattn_head = operands
        query_f = query_head.astype(jnp.float32)
        key_f = key_head.astype(jnp.float32)
        value_f = value_head.astype(jnp.float32)
        dattn_f = dattn_head.astype(jnp.float32)
        query_blk = query_f.reshape(NBLK, BLOCK, HEAD_DIM)
        key_win = window_view(key_f)
        value_win = window_view(value_f)
        key_glob = key_f[global_pos]
        value_glob = value_f[global_pos]
        win_scores = jnp.einsum('bid,brjd->birj', query_blk, key_win, precision=exact_prec) * score_scale
        win_scores = jnp.where(pair_ok, win_scores, -jnp.inf)
        glob_scores = jnp.einsum('bid,gd->big', query_blk, key_glob, precision=exact_prec) * score_scale
        row_peak = jnp.maximum(lax.optimization_barrier(jnp.max(win_scores, axis=(2, 3))), lax.optimization_barrier(jnp.max(glob_scores, axis=2)))
        row_mass = lax.optimization_barrier(jnp.sum(jnp.exp(win_scores - row_peak[:, :, None, None]), axis=(2, 3))) + lax.optimization_barrier(jnp.sum(jnp.exp(glob_scores - row_peak[:, :, None]), axis=2))
        row_lse = row_peak + jnp.log(row_mass)
        win_prob = jnp.exp(win_scores - row_lse[:, :, None, None])
        glob_prob = jnp.exp(glob_scores - row_lse[:, :, None])
        win_weight = rounded(win_prob)
        glob_weight = rounded(glob_prob)
        attn_win = jnp.einsum('birj,brjd->bid', win_weight, value_win, precision=exact_prec) + jnp.einsum('big,gd->bid', glob_weight, value_glob, precision=exact_prec)
        attn_win = attn_win.reshape(TOKENS, HEAD_DIM)
        query_rows = query_f[global_pos]
        row_scores = jnp.dot(query_rows, key_f.T, precision=exact_prec) * score_scale
        rows_peak = lax.optimization_barrier(jnp.max(row_scores, axis=1))
        rows_lse = rows_peak + jnp.log(lax.optimization_barrier(jnp.sum(jnp.exp(row_scores - rows_peak[:, None]), axis=1)))
        row_prob = jnp.exp(row_scores - rows_lse[:, None])
        attn_rows = jnp.dot(row_prob, value_f, precision=exact_prec)
        attn_bf = attn_win.at[global_pos].set(attn_rows).astype(jnp.bfloat16)
        attn_f = lax.optimization_barrier(attn_bf).astype(jnp.float32)
        dattn_win = jnp.where(is_global[:, None], 0.0, dattn_f)
        delta_win = lax.optimization_barrier(jnp.sum(dattn_win * attn_f, axis=1)).reshape(NBLK, BLOCK)
        dattn_blk = dattn_win.reshape(NBLK, BLOCK, HEAD_DIM)
        win_dprob = jnp.einsum('bid,brjd->birj', dattn_blk, value_win, precision=exact_prec)
        glob_dprob = jnp.einsum('bid,gd->big', dattn_blk, value_glob, precision=exact_prec)
        win_dscore = rounded(win_prob * (win_dprob - delta_win[:, :, None, None]))
        glob_dscore = rounded(glob_prob * (glob_dprob - delta_win[:, :, None]))
        dq_win = jnp.einsum('birj,brjd->bid', win_dscore, key_win, precision=exact_prec) + jnp.einsum('big,gd->bid', glob_dscore, key_glob, precision=exact_prec)
        dq_win = dq_win.reshape(TOKENS, HEAD_DIM)
        dk_win = window_fold(jnp.einsum('birj,bid->brjd', win_dscore, query_blk, precision=exact_prec))
        dk_win = dk_win.at[global_pos].add(jnp.einsum('big,bid->gd', glob_dscore, query_blk, precision=exact_prec))
        dv_win = window_fold(jnp.einsum('birj,bid->brjd', win_weight, dattn_blk, precision=exact_prec))
        dv_win = dv_win.at[global_pos].add(jnp.einsum('big,bid->gd', glob_weight, dattn_blk, precision=exact_prec))
        dattn_rows = dattn_f[global_pos]
        delta_rows = lax.optimization_barrier(jnp.sum(dattn_rows * attn_f[global_pos], axis=1))
        row_dprob = jnp.dot(dattn_rows, value_f.T, precision=exact_prec)
        row_dscore = rounded(row_prob * (row_dprob - delta_rows[:, None]))
        row_weight = rounded(row_prob)
        grad_q = dq_win.at[global_pos].add(jnp.dot(row_dscore, key_f, precision=exact_prec)) * score_scale
        grad_k = (dk_win + jnp.dot(row_dscore.T, query_rows, precision=exact_prec)) * score_scale
        grad_v = dv_win + jnp.dot(row_weight.T, dattn_rows, precision=exact_prec)
        return (attn_bf, grad_q.astype(jnp.bfloat16), grad_k.astype(jnp.bfloat16), grad_v.astype(jnp.bfloat16))

    def split_heads(matrix):
        return matrix.reshape(TOKENS, HEADS, HEAD_DIM).transpose(1, 0, 2)

    def merge_heads(stacked):
        return stacked.transpose(1, 0, 2).reshape(TOKENS, D)
    attn_all, grad_q_all, grad_k_all, grad_v_all = lax.map(one_head, (split_heads(queries), split_heads(keys), split_heads(values), split_heads(d_attn)))
    layer_out = jnp.dot(merge_heads(attn_all), out_weight, preferred_element_type=jnp.float32).astype(jnp.bfloat16)
    return (layer_out, merge_heads(grad_q_all), merge_heads(grad_k_all), merge_heads(grad_v_all))
```

```python
import math

import jax
import jax.numpy as jnp
from jax import lax
from jax.experimental import pallas as pl
from jax.experimental.pallas import tpu as pltpu
from jax.sharding import PartitionSpec as P

HEAD_DIM = 128
BLOCK = 128
WBLK = 4
RIM = (WBLK - 1) * BLOCK
QROWS = 2 * BLOCK
SCALE = 1.0 / math.sqrt(HEAD_DIM)
SCALE2 = SCALE * math.log2(math.e)
BF = jnp.bfloat16
F32 = jnp.float32
NEG = float("-inf")


def nn(a, b):
    return lax.dot_general(a, b, (((1,), (0,)), ((), ())), preferred_element_type=F32)


def nt(a, b):
    return lax.dot_general(a, b, (((1,), (1,)), ((), ())), preferred_element_type=F32)


def tn(a, b):
    return lax.dot_general(a, b, (((0,), (0,)), ((), ())), preferred_element_type=F32)


def rows(slot, count):
    return pl.ds(pl.multiple_of(slot * count, count), count)


def local_call(name, body, ids, arrays, outs, scratch=(), flops=0):
    moved = sum(a.size * a.dtype.itemsize for a in arrays)
    moved += sum(math.prod(s) * jnp.dtype(t).itemsize for s, t in outs)
    return pl.pallas_call(
        body,
        name=name,
        out_shape=tuple(jax.ShapeDtypeStruct(s, t) for s, t in outs),
        in_specs=[pl.BlockSpec(memory_space=pltpu.SMEM)]
        + [pl.BlockSpec(memory_space=pltpu.VMEM)] * len(arrays),
        out_specs=tuple(pl.BlockSpec(memory_space=pltpu.VMEM) for _ in outs),
        scratch_shapes=list(scratch),
        compiler_params=pltpu.CompilerParams(vmem_limit_bytes=40 * 2**20),
        cost_estimate=pl.CostEstimate(flops=flops, bytes_accessed=moved, transcendentals=0),
    )(ids, *arrays)


def pack_kv_body(ids, k, v, mask, *outs):
    tok = k.shape[0]
    for i, out in enumerate(outs):
        col = rows(ids[0] ^ i, HEAD_DIM)
        out[0:tok, :] = k[:, col]
        out[tok : 2 * tok, :] = v[:, col]
        out[2 * tok :, :] = mask[...]


def pack_qo_body(ids, q, out_grad, out_weight, *refs):
    outs, d_attn = refs[:-1], refs[-1]
    tok = q.shape[0]
    d_attn[...] = nt(out_grad[...], out_weight[...]).astype(BF)
    for i, out in enumerate(outs):
        col = rows(ids[0] ^ i, HEAD_DIM)
        out[0:tok, :] = q[:, col]
        out[tok:, :] = d_attn[:, col]


def pick_rows(pos_col, tok):
    hits = pos_col == lax.broadcasted_iota(jnp.int32, (pos_col.shape[0], tok), 1)
    return hits.astype(BF)


def place_rows(pos_row, tok):
    return lax.broadcasted_iota(jnp.int32, (tok, pos_row.shape[1]), 0) == pos_row


def join_kv_body(ids, pos_col, *refs):
    pieces, (k, v, bias, picked, rim) = refs[:-5], refs[-5:]
    tok = k.shape[0] // len(pieces)
    n_rows = bias.shape[0] // len(pieces)
    for i, piece in enumerate(pieces):
        slot = ids[0] ^ i
        k[rows(slot, tok), :] = piece[0:tok, :]
        v[rows(slot, tok), :] = piece[tok : 2 * tok, :]
        open_ = piece[2 * tok :, :].astype(F32)
        entry = lax.broadcasted_iota(jnp.int32, open_.shape, 0) + slot * n_rows
        inside = (ids[1] > 0) | (entry // WBLK >= entry % WBLK)
        bias[rows(slot, n_rows), :] = jnp.where((open_ > 0.5) & inside, 0.0, NEG)
    picks = pick_rows(pos_col[...], tok)
    n = pos_col.shape[0]
    picked[0:n, :] = nn(picks, k[0:tok, :]).astype(BF)
    picked[n:, :] = nn(picks, v[0:tok, :]).astype(BF)
    rim[0:RIM, :] = k[k.shape[0] - RIM :, :]
    rim[RIM:, :] = v[k.shape[0] - RIM :, :]


def join_qo_body(ids, pos_col, pos_row, *refs):
    pieces, (q, d_attn, picked) = refs[:-3], refs[-3:]
    tok = q.shape[0] // len(pieces)
    for i, piece in enumerate(pieces):
        slot = ids[0] ^ i
        q[rows(slot, tok), :] = piece[0:tok, :]
        d_attn[rows(slot, tok), :] = piece[tok:, :]
    picks = pick_rows(pos_col[...], tok)
    n = pos_col.shape[0]
    picked[0:n, :] = nn(picks, q[0:tok, :]).astype(BF)
    picked[n:, :] = nn(picks, d_attn[0:tok, :]).astype(BF)

    @pl.when(ids[1] == 0)
    def _():
        hit = place_rows(pos_row[...], tok).astype(F32)
        is_row = jnp.max(hit, axis=1, keepdims=True) > 0.5
        kept = jnp.where(is_row, 0.0, d_attn[0:tok, :].astype(F32))
        d_attn[0:tok, :] = kept.astype(BF)


def row_forward_body(ids, qo, k, v, attn_t, stats, scores):
    n = qo.shape[0] // 2
    step = 512
    query, d_out = qo[0:n, :], qo[n:, :]
    peak = None
    for c in range(0, k.shape[0], step):
        s = nt(k[c : c + step, :], query) * SCALE2
        scores[c : c + step, :] = s
        top = jnp.max(s, axis=0, keepdims=True)
        peak = top if peak is None else jnp.maximum(peak, top)
    mass = jnp.zeros((1, n), F32)
    dot = jnp.zeros((1, n), F32)
    numer = jnp.zeros((HEAD_DIM, n), F32)
    for c in range(0, k.shape[0], step):
        e = jnp.exp2(scores[c : c + step, :] - peak)
        vals = v[c : c + step, :]
        mass = mass + jnp.sum(e, axis=0, keepdims=True)
        dot = dot + jnp.sum(e * nt(vals, d_out), axis=0, keepdims=True)
        numer = numer + tn(vals, e.astype(BF))
    attn_t[...] = (numer / mass).astype(BF)
    stats[...] = jnp.concatenate([peak, mass, dot, jnp.zeros((5, n), F32)], axis=0)


def merged(mine, other):
    peak = jnp.maximum(mine[0:1, :], other[0:1, :])
    wa = jnp.exp2(mine[0:1, :] - peak)
    wb = jnp.exp2(other[0:1, :] - peak)
    mass = mine[1:2, :] * wa + other[1:2, :] * wb
    dot = mine[2:3, :] * wa + other[2:3, :] * wb
    return peak, mass, dot, mine[1:2, :] * wa / mass, other[1:2, :] * wb / mass


def window_body(ids, pos_row, q, d_out, k, v, rim, kv_glob, bias, *refs):
    attn, dq, dk, dv, rim_back, dk_glob, dv_glob, kx, vx, kt, vt, key_bias = refs
    n = kv_glob.shape[0] // 2
    total = k.shape[0]
    tok = total // 4
    kx[0:RIM, :] = rim[0:RIM, :]
    kx[RIM:, :] = k[...]
    vx[0:RIM, :] = rim[RIM:, :]
    vx[RIM:, :] = v[...]
    kt[...] = kx[...].T
    vt[...] = vx[...].T
    dk[...] = jnp.zeros_like(dk)
    dv[...] = jnp.zeros_like(dv)
    dk_glob[...] = jnp.zeros_like(dk_glob)
    dv_glob[...] = jnp.zeros_like(dv_glob)
    key_bias[...] = jnp.zeros_like(key_bias)

    @pl.when(ids[1] == 0)
    def _():
        hit = place_rows(pos_row[...], tok).astype(F32)
        is_row = jnp.max(hit, axis=1, keepdims=True) > 0.5
        key_bias[RIM : RIM + tok, :] = jnp.where(is_row, NEG, jnp.zeros((tok, QROWS), F32))

    kg, vg = kv_glob[0:n, :], kv_glob[n:, :]
    kgt, vgt = kg.T, vg.T
    key_in = lax.broadcasted_iota(jnp.int32, (BLOCK, QROWS), 0)
    query_in = lax.broadcasted_iota(jnp.int32, (BLOCK, QROWS), 1)
    n_keys = RIM + QROWS
    shut = jnp.full((1, BLOCK), NEG, F32)

    def step(sb, carry):
        here = rows(sb, QROWS)
        span = pl.ds(pl.multiple_of(sb * QROWS, QROWS), n_keys)
        qb, dob = q[here, :], d_out[here, :]
        kw, vw = kx[span, :], vx[span, :]
        raw = nt(kw, qb)
        parts = []
        for kb in range(n_keys // BLOCK):
            halves = []
            for half in range(QROWS // BLOCK):
                r = half + WBLK - 1 - kb
                if 0 <= r < WBLK:
                    at = (sb * (QROWS // BLOCK) + half) * WBLK + r
                    halves.append(bias[pl.ds(at, 1), :])
                else:
                    halves.append(shut)
            part = (
                raw[kb * BLOCK : (kb + 1) * BLOCK, :] * SCALE2
                + key_bias[pl.ds(pl.multiple_of(sb * QROWS + kb * BLOCK, BLOCK), BLOCK), :]
                + jnp.concatenate(halves, axis=1)
            )
            own = kb - (WBLK - 1)
            if own >= 0:
                part = jnp.where(query_in - key_in >= own * BLOCK, part, NEG) if own else jnp.where(
                    key_in <= query_in, part, NEG
                )
            parts.append(part)
        tw = jnp.concatenate(parts, axis=0)
        tg = nt(kg, qb) * SCALE2
        peak = jnp.maximum(
            jnp.max(tw, axis=0, keepdims=True), jnp.max(tg, axis=0, keepdims=True)
        )
        ew, eg = jnp.exp2(tw - peak), jnp.exp2(tg - peak)
        mass = jnp.sum(ew, axis=0, keepdims=True) + jnp.sum(eg, axis=0, keepdims=True)
        inv = 1.0 / mass
        pw, pg = ew * inv, eg * inv
        ww, wg = pw.astype(BF), pg.astype(BF)
        out_t = (nn(vt[:, span], ww) + nn(vgt, wg)).astype(BF).astype(F32)
        attn[here, :] = out_t.T.astype(BF)
        delta = jnp.sum(out_t * dob.astype(F32).T, axis=0, keepdims=True)
        dw = (pw * (nt(vw, dob) - delta)).astype(BF)
        dg = (pg * (nt(vg, dob) - delta)).astype(BF)
        dq_t = nn(kt[:, span], dw) + nn(kgt, dg)
        dq[here, :] = (dq_t.T * SCALE).astype(BF)
        dk[span, :] += nn(dw, qb)
        dv[span, :] += nn(ww, dob)
        dk_glob[...] += nn(dg, qb)
        dv_glob[...] += nn(wg, dob)
        return carry

    lax.fori_loop(0, total // QROWS, step, 0)
    rim_back[0:RIM, :] = dk[0:RIM, :].astype(BF)
    rim_back[RIM:, :] = dv[0:RIM, :].astype(BF)


def row_backward_body(ids, qo, k, v, stats, other, dkw, dvw, dkg, dvg, dk, dv, sums):
    n = qo.shape[0] // 2
    step = 512
    query, d_out = qo[0:n, :], qo[n:, :]
    peak, mass, dot, _, _ = merged(stats[...], other[...])
    lse = peak + jnp.log2(mass)
    delta = dot / mass
    dq_t = jnp.zeros((HEAD_DIM, n), F32)
    for c in range(0, k.shape[0], step):
        keys, vals = k[c : c + step, :], v[c : c + step, :]
        prob = jnp.exp2(nt(keys, query) * SCALE2 - lse)
        ds = (prob * (nt(vals, d_out) - delta)).astype(BF)
        dk[c : c + step, :] = dkw[RIM + c : RIM + c + step, :] + nn(ds, query)
        dv[c : c + step, :] = dvw[RIM + c : RIM + c + step, :] + nn(prob.astype(BF), d_out)
        dq_t = dq_t + tn(keys, ds)
    sums[0:n, :] = dq_t.T.astype(BF)
    sums[n : 2 * n, :] = dkg[...].astype(BF)
    sums[2 * n :, :] = dvg[...].astype(BF)


def pack_attn_body(ids, pos_row, attn, mine_t, other_t, stats, other, *refs):
    outs, full = refs[:-1], refs[-1]
    tok = attn.shape[0] // len(outs)
    full[...] = attn[...]

    @pl.when(ids[1] == 0)
    def _():
        _, _, _, wa, wb = merged(stats[...], other[...])
        both_t = (mine_t[...].astype(F32) * wa + other_t[...].astype(F32) * wb).astype(BF)
        hit = place_rows(pos_row[...], tok)
        is_row = jnp.max(hit.astype(F32), axis=1, keepdims=True) > 0.5
        placed = nt(hit.astype(BF), both_t)
        full[0:tok, :] = jnp.where(is_row, placed, attn[0:tok, :].astype(F32)).astype(BF)

    for i, out in enumerate(outs):
        out[...] = full[rows(ids[0] ^ i, tok), :]


def project_body(ids, w, *refs):
    pieces, (keep, send, attn) = refs[:-3], refs[-3:]
    for i, piece in enumerate(pieces):
        attn[:, rows(ids[0] ^ i, HEAD_DIM)] = piece[...]
    cols = keep.shape[2]
    a = attn[...]
    me = ids[2]
    for i, group in enumerate((me, me ^ 2)):
        keep[i] = nn(a, w[:, rows(group, cols)]).astype(BF)
    for i, group in enumerate((me ^ 1, me ^ 3)):
        send[i] = nn(a, w[:, rows(group, cols)]).astype(BF)


def pack_grads_body(ids, pos_row, dq, dk, dv, rim_back, sums, other, *refs):
    outs, (dqf, dkf, dvf) = refs[:-3], refs[-3:]
    total = dq.shape[0]
    tok = total // len(outs)
    n = sums.shape[0] // 3
    dqf[...] = dq[...]
    dkf[...] = dk[...]
    dvf[...] = dv[...]
    dkf[total - RIM :, :] += rim_back[0:RIM, :].astype(F32)
    dvf[total - RIM :, :] += rim_back[RIM:, :].astype(F32)

    @pl.when(ids[1] == 0)
    def _():
        both = sums[...].astype(F32) + other[...].astype(F32)
        hit = place_rows(pos_row[...], tok).astype(BF)
        dq_add = nn(hit, (both[0:n, :] * SCALE).astype(BF))
        dqf[0:tok, :] = (dqf[0:tok, :].astype(F32) + dq_add).astype(BF)
        dkf[0:tok, :] += nn(hit, both[n : 2 * n, :].astype(BF))
        dvf[0:tok, :] += nn(hit, both[2 * n :, :].astype(BF))

    for i, out in enumerate(outs):
        here = rows(ids[0] ^ i, tok)
        out[0:tok, :] = dqf[here, :]
        out[tok : 2 * tok, :] = (dkf[here, :] * SCALE).astype(BF)
        out[2 * tok :, :] = dvf[here, :].astype(BF)


def join_grads_body(ids, *refs):
    pieces, outs = refs[:-3], refs[-3:]
    tok = outs[0].shape[0]
    for i, piece in enumerate(pieces):
        col = rows(ids[0] ^ i, HEAD_DIM)
        for at, out in enumerate(outs):
            out[:, col] = piece[at * tok : (at + 1) * tok, :]


def on_device(queries, keys, values, out_weight, out_grad, global_pos, block_mask):
    tok, cols = queries.shape
    heads = cols // HEAD_DIM
    n_seq = lax.axis_size("seq")
    n_groups = n_seq // heads
    total = heads * tok
    n_glob = global_pos.shape[0]
    seq_index = lax.axis_index("seq")
    group = seq_index // heads
    ids = jnp.stack([seq_index % heads, group, lax.axis_index("head")]).astype(jnp.int32)
    pos_col = global_pos.reshape(n_glob, 1)
    pos_row = global_pos.reshape(1, n_glob)

    def swap_in_group(pieces):
        moved = [
            lax.ppermute(piece, "seq", [(s, s ^ i) for s in range(n_seq)])
            for i, piece in enumerate(pieces)
            if i
        ]
        return [pieces[0]] + moved

    def from_first(x):
        d = 1
        while d < n_groups:
            route = [
                (g * heads + j, (g + d) * heads + j)
                for g in range(d)
                for j in range(heads)
                if g + d < n_groups
            ]
            x = jnp.where((group >= d) & (group < 2 * d), lax.ppermute(x, "seq", route), x)
            d *= 2
        return x

    def to_next_group(x, step):
        route = [(s, s + step * heads) for s in range(n_seq) if 0 <= s + step * heads < n_seq]
        return lax.ppermute(x, "seq", route)

    def with_group(x, d):
        return lax.ppermute(x, "seq", [(s, s ^ (d * heads)) for s in range(n_seq)])

    mask_rows = jnp.broadcast_to(
        block_mask.reshape(-1, 1).astype(BF), (block_mask.size, HEAD_DIM)
    )
    kv_rows = 2 * tok + block_mask.size
    kv = swap_in_group(
        local_call(
            "pack_kv", pack_kv_body, ids, (keys, values, mask_rows), [((kv_rows, HEAD_DIM), BF)] * heads
        )
    )
    qo = swap_in_group(
        local_call(
            "pack_qo",
            pack_qo_body,
            ids,
            (queries, out_grad, out_weight),
            [((2 * tok, HEAD_DIM), BF)] * heads,
            [pltpu.VMEM((tok, cols), BF)],
            flops=2 * tok * cols * out_weight.shape[1],
        )
    )
    k, v, bias, kv_pick, rim_out = local_call(
        "join_kv",
        join_kv_body,
        ids,
        (pos_col, *kv),
        [
            ((total, HEAD_DIM), BF),
            ((total, HEAD_DIM), BF),
            ((heads * block_mask.size, HEAD_DIM), F32),
            ((2 * n_glob, HEAD_DIM), BF),
            ((2 * RIM, HEAD_DIM), BF),
        ],
    )
    rim = to_next_group(rim_out, 1)
    kv_glob = from_first(kv_pick)
    q, d_attn, qo_pick = local_call(
        "join_qo",
        join_qo_body,
        ids,
        (pos_col, pos_row, *qo),
        [
            ((total, HEAD_DIM), BF),
            ((total, HEAD_DIM), BF),
            ((2 * n_glob, HEAD_DIM), BF),
        ],
    )
    qo_glob = from_first(qo_pick)
    row_flops = 2 * n_glob * total * HEAD_DIM
    attn_t, stats = local_call(
        "row_forward",
        row_forward_body,
        ids,
        (qo_glob, k, v),
        [((HEAD_DIM, n_glob), BF), ((8, n_glob), F32)],
        [pltpu.VMEM((total, n_glob), F32)],
        flops=3 * row_flops,
    )
    d = 1
    while 2 * d < n_groups:
        other_t, other = with_group(attn_t, d), with_group(stats, d)
        peak, mass, dot, wa, wb = merged(stats, other)
        attn_t = (attn_t.astype(F32) * wa + other_t.astype(F32) * wb).astype(BF)
        stats = jnp.concatenate([peak, mass, dot, jnp.zeros((5, n_glob), F32)], axis=0)
        d *= 2
    other_t, other = with_group(attn_t, d), with_group(stats, d)
    wide = RIM + total
    attn, dq, dkw, dvw, rim_sum, dkg, dvg = local_call(
        "window",
        window_body,
        ids,
        (pos_row, q, d_attn, k, v, rim, kv_glob, bias),
        [
            ((total, HEAD_DIM), BF),
            ((total, HEAD_DIM), BF),
            ((wide, HEAD_DIM), F32),
            ((wide, HEAD_DIM), F32),
            ((2 * RIM, HEAD_DIM), BF),
            ((n_glob, HEAD_DIM), F32),
            ((n_glob, HEAD_DIM), F32),
        ],
        [
            pltpu.VMEM((wide, HEAD_DIM), BF),
            pltpu.VMEM((wide, HEAD_DIM), BF),
            pltpu.VMEM((HEAD_DIM, wide), BF),
            pltpu.VMEM((HEAD_DIM, wide), BF),
            pltpu.VMEM((wide, QROWS), F32),
        ],
        flops=12 * total * (RIM + QROWS + n_glob) * HEAD_DIM,
    )
    rim_back = to_next_group(rim_sum, -1)
    attn_parts = swap_in_group(
        local_call(
            "pack_attn",
            pack_attn_body,
            ids,
            (pos_row, attn, attn_t, other_t, stats, other),
            [((tok, HEAD_DIM), BF)] * heads,
            [pltpu.VMEM((total, HEAD_DIM), BF)],
        )
    )
    dk, dv, sums = local_call(
        "row_backward",
        row_backward_body,
        ids,
        (qo_glob, k, v, stats, other, dkw, dvw, dkg, dvg),
        [
            ((total, HEAD_DIM), F32),
            ((total, HEAD_DIM), F32),
            ((3 * n_glob, HEAD_DIM), BF),
        ],
        flops=5 * row_flops,
    )

    def to_lower(x, d):
        route = [
            (g * heads + j, (g - d) * heads + j)
            for g in range(d, min(2 * d, n_groups))
            for j in range(heads)
        ]
        return lax.ppermute(x, "seq", route)

    d = n_groups // 2
    while d > 1:
        sums = (sums.astype(F32) + to_lower(sums, d).astype(F32)).astype(BF)
        d //= 2
    other_sums = to_lower(sums, 1)
    n_head = lax.axis_size("head")
    out_cols = out_weight.shape[1] // n_head
    keep, send = local_call(
        "project",
        project_body,
        ids,
        (out_weight, *attn_parts),
        [((2, tok, out_cols), BF)] * 2,
        [pltpu.VMEM((tok, cols), BF)],
        flops=2 * tok * cols * out_weight.shape[1],
    )
    half = lax.ppermute(send, "head", [(h, h ^ 1) for h in range(n_head)])
    summed = keep.astype(F32) + half.astype(F32)
    far = lax.ppermute(summed[1].astype(BF), "head", [(h, h ^ 2) for h in range(n_head)])
    layer_out = (summed[0] + far.astype(F32)).astype(BF)
    grads = swap_in_group(
        local_call(
            "pack_grads",
            pack_grads_body,
            ids,
            (pos_row, dq, dk, dv, rim_back, sums, other_sums),
            [((3 * tok, HEAD_DIM), BF)] * heads,
            [
                pltpu.VMEM((total, HEAD_DIM), BF),
                pltpu.VMEM((total, HEAD_DIM), F32),
                pltpu.VMEM((total, HEAD_DIM), F32),
            ],
        )
    )
    grad_queries, grad_keys, grad_values = local_call(
        "join_grads", join_grads_body, ids, tuple(grads), [((tok, cols), BF)] * 3
    )
    return (layer_out, grad_queries, grad_keys, grad_values)


def solution(mesh):
    return jax.shard_map(
        on_device,
        mesh=mesh,
        in_specs=(
            P("seq", "head"),
            P("seq", "head"),
            P("seq", "head"),
            P("head", None),
            P("seq", None),
            P(),
            P("seq", None),
        ),
        out_specs=(P("seq", "head"), P("seq", "head"), P("seq", "head"), P("seq", "head")),
        check_vma=False,
    )
```

```python
import functools
import math

import jax
import jax.numpy as jnp
from jax import lax
from jax.experimental import pallas as pl
from jax.experimental.pallas import tpu as pltpu
from jax.sharding import PartitionSpec as P

HEAD_DIM = 128
BLOCK = 128
WBLK = 4
RIM = (WBLK - 1) * BLOCK
QROWS = 2 * BLOCK
SCALE = 1.0 / math.sqrt(HEAD_DIM)
SCALE2 = SCALE * math.log2(math.e)
BF = jnp.bfloat16
F32 = jnp.float32
NEG = float("-inf")
JOIN_US = 12.0
PACK_MIB = 14


def nn(a, b):
    return lax.dot_general(a, b, (((1,), (0,)), ((), ())), preferred_element_type=F32)


def nt(a, b):
    return lax.dot_general(a, b, (((1,), (1,)), ((), ())), preferred_element_type=F32)


def tn(a, b):
    return lax.dot_general(a, b, (((0,), (0,)), ((), ())), preferred_element_type=F32)


def rows(slot, count):
    return pl.ds(pl.multiple_of(slot * count, count), count)


def local_call(name, body, ids, arrays, outs, scratch=(), after=(), aliases=None, far=(), mib=14, us=0.0, out_space=pltpu.VMEM):
    first = 1 + len(arrays) + len(far)

    def kernel(*refs):
        body(*refs[:first], *refs[first + len(after) :])

    return pl.pallas_call(
        kernel,
        name=name,
        out_shape=tuple(jax.ShapeDtypeStruct(s, t) for s, t in outs),
        in_specs=[pl.BlockSpec(memory_space=pltpu.SMEM)]
        + [pl.BlockSpec(memory_space=pltpu.VMEM)] * len(arrays)
        + [pl.BlockSpec(memory_space=space) for _, space in far]
        + [pl.BlockSpec(memory_space=pl.ANY)] * len(after),
        out_specs=tuple(pl.BlockSpec(memory_space=out_space) for _ in outs),
        scratch_shapes=list(scratch),
        compiler_params=pltpu.CompilerParams(vmem_limit_bytes=mib * 2**20),
        input_output_aliases=aliases or {},
        cost_estimate=pl.CostEstimate(
            flops=1000 + int(us * 1.15e9), bytes_accessed=1000, transcendentals=0
        ),
    )(ids, *arrays, *[array for array, _ in far], *after)


def pack_kv_body(ids, k, v, *refs):
    outs, sems = refs[:-1], refs[-1]
    tok = k.shape[0]
    copies = []
    for i, out in enumerate(outs):
        col = rows(ids[0] ^ i, HEAD_DIM)
        copies += [
            pltpu.make_async_copy(k.at[:, col], out.at[0:tok, :], sems.at[2 * i]),
            pltpu.make_async_copy(v.at[:, col], out.at[tok:, :], sems.at[2 * i + 1]),
        ]
    for copy in copies:
        copy.start()
    for copy in copies:
        copy.wait()


def pack_qo_body(ids, q, out_grad, out_weight, block_mask, *refs):
    outs, d_attn = refs[:-1], refs[-1]
    tok = q.shape[0]
    entries = outs[0].shape[0] - 2 * tok
    at = lax.broadcasted_iota(jnp.int32, (entries, HEAD_DIM), 0)
    mask = jnp.zeros((entries, HEAD_DIM), jnp.int32)
    for e in range(entries):
        mask = jnp.where(at == e, block_mask[e // WBLK, e % WBLK], mask)
    mask = mask.astype(F32).astype(BF)
    d_attn[...] = nt(out_grad[...], out_weight[...]).astype(BF)
    for i, out in enumerate(outs):
        col = rows(ids[0] ^ i, HEAD_DIM)
        out[0:tok, :] = q[:, col]
        out[tok : 2 * tok, :] = d_attn[:, col]
        out[2 * tok :, :] = mask


def pick_rows(pos_col, tok):
    hits = pos_col == lax.broadcasted_iota(jnp.int32, (pos_col.shape[0], tok), 1)
    return hits.astype(BF)


def place_rows(pos_row, tok):
    return lax.broadcasted_iota(jnp.int32, (tok, pos_row.shape[1]), 0) == pos_row


def row_column(pos_row, tok):
    hit = place_rows(pos_row, tok).astype(F32)
    return jnp.max(hit, axis=1, keepdims=True) > 0.5


def join_kv_body(ids, pos_col, pos_row, *refs):
    pieces, (k, v, key_bias, picked, rim) = refs[:-5], refs[-5:]
    tok = k.shape[0] // len(pieces)
    for i, piece in enumerate(pieces):
        slot = ids[0] ^ i
        k[rows(slot, tok), :] = piece[0:tok, :]
        v[rows(slot, tok), :] = piece[tok:, :]
    picks = pick_rows(pos_col[...], tok)
    n = pos_col.shape[0]
    picked[0:n, :] = nn(picks, k[0:tok, :]).astype(BF)
    picked[n:, :] = nn(picks, v[0:tok, :]).astype(BF)
    rim[0:RIM, :] = k[k.shape[0] - RIM :, :]
    rim[RIM:, :] = v[k.shape[0] - RIM :, :]
    hidden = jnp.logical_and(row_column(pos_row[...], tok), ids[1] == 0)
    key_bias[...] = jnp.where(hidden, NEG, jnp.zeros(key_bias.shape, F32))


def join_qo_body(ids, pos_col, pos_row, *refs):
    pieces, (q, d_attn, bias, picked) = refs[:-4], refs[-4:]
    tok = q.shape[0] // len(pieces)
    n_rows = bias.shape[0] // len(pieces)
    n = pos_col.shape[0]
    for i, piece in enumerate(pieces):
        slot = ids[0] ^ i
        q[rows(slot, tok), :] = piece[0:tok, :]
        d_attn[rows(slot, tok), :] = piece[tok : 2 * tok, :]
        open_ = piece[2 * tok :, :].astype(F32)
        entry = lax.broadcasted_iota(jnp.int32, open_.shape, 0) + slot * n_rows
        inside = (ids[1] > 0) | (entry // WBLK >= entry % WBLK)
        bias[rows(slot, n_rows), :] = jnp.where((open_ > 0.5) & inside, 0.0, NEG)

    @pl.when(ids[1] == 0)
    def _():
        picks = pick_rows(pos_col[...], tok)
        picked[0:n, :] = nn(picks, q[0:tok, :]).astype(BF)
        picked[n:, :] = nn(picks, d_attn[0:tok, :]).astype(BF)
        is_row = row_column(pos_row[...], tok)
        kept = jnp.where(is_row, 0.0, d_attn[0:tok, :].astype(F32))
        d_attn[0:tok, :] = kept.astype(BF)

    @pl.when(ids[1] > 0)
    def _():
        picked[...] = jnp.zeros_like(picked)


def row_forward_body(ids, picked, k, v, mine, scores):
    n = picked.shape[0] // 2
    step = 512
    query, d_out = picked[0:n, :], picked[n:, :]
    peak = None
    for c in range(0, k.shape[0], step):
        s = nt(k[c : c + step, :], query) * SCALE2
        scores[c : c + step, :] = s
        top = jnp.max(s, axis=0, keepdims=True)
        peak = top if peak is None else jnp.maximum(peak, top)
    mass = jnp.zeros((1, n), F32)
    dot = jnp.zeros((1, n), F32)
    numer = jnp.zeros((HEAD_DIM, n), F32)
    for c in range(0, k.shape[0], step):
        e = jnp.exp2(scores[c : c + step, :] - peak)
        vals = v[c : c + step, :]
        mass = mass + jnp.sum(e, axis=0, keepdims=True)
        dot = dot + jnp.sum(e * nt(vals, d_out), axis=0, keepdims=True)
        numer = numer + tn(vals, e.astype(BF))
    mine[0:HEAD_DIM, :] = (numer / mass).astype(BF)
    mine[HEAD_DIM:, :] = in_thirds((peak, mass, dot))


def in_thirds(values):
    parts = []
    for value in values:
        for _ in range(3):
            part = value.astype(BF).astype(F32)
            parts.append(part)
            value = value - part
    empty = jnp.zeros((16 - len(parts), parts[0].shape[1]), F32)
    return jnp.concatenate(parts + [empty], axis=0).astype(BF)


def merged(mine, other):
    thirds = [ref[HEAD_DIM:, :].astype(F32) for ref in (mine, other)]
    (pa, ma, da), (pb, mb, db) = [
        [t[3 * i : 3 * i + 1] + t[3 * i + 1 : 3 * i + 2] + t[3 * i + 2 : 3 * i + 3] for i in range(3)]
        for t in thirds
    ]
    peak = jnp.maximum(pa, pb)
    wa, wb = jnp.exp2(pa - peak), jnp.exp2(pb - peak)
    mass = ma * wa + mb * wb
    return peak, mass, da * wa + db * wb, ma * wa / mass, mb * wb / mass


def merged_attn(mine, other, wa, wb):
    both = mine[0:HEAD_DIM, :].astype(F32) * wa + other[0:HEAD_DIM, :].astype(F32) * wb
    return both.astype(BF)


def merge_body(ids, mine, other, out):
    peak, mass, dot, wa, wb = merged(mine, other)
    out[0:HEAD_DIM, :] = merged_attn(mine, other, wa, wb)
    out[HEAD_DIM:, :] = in_thirds((peak, mass, dot))


N_KEYS = RIM + QROWS


def window_keys(sb, k, v, rim):
    first = sb * QROWS - RIM
    cut = max(0, -first)
    inner = slice(first + cut, (sb + 1) * QROWS)
    kw, vw = k[inner, :], v[inner, :]
    if cut:
        kw = jnp.concatenate([rim[RIM - cut : RIM, :], kw], axis=0)
        vw = jnp.concatenate([rim[2 * RIM - cut :, :], vw], axis=0)
    return first, cut, inner, kw, vw


def window_forward_body(steps, with_rim, ids, *refs):
    q, d_out, k, v, picked, bias, key_bias = refs[:7]
    rim = refs[7] if with_rim else None
    attn, weights, delta = refs[-3:]
    n = picked.shape[0] // 2
    kg, vg = picked[0:n, :], picked[n:, :]
    key_in = lax.broadcasted_iota(jnp.int32, (BLOCK, QROWS), 0)
    query_in = lax.broadcasted_iota(jnp.int32, (BLOCK, QROWS), 1)
    shut = jnp.full((1, BLOCK), NEG, F32)
    for sb in steps:
        here = slice(sb * QROWS, (sb + 1) * QROWS)
        first, _, _, kw, vw = window_keys(sb, k, v, rim)
        qb = q[here, :]
        raw = nt(kw, qb)
        parts = []
        for kb in range(N_KEYS // BLOCK):
            halves = []
            for half in range(QROWS // BLOCK):
                r = half + WBLK - 1 - kb
                at = (sb * (QROWS // BLOCK) + half) * WBLK + r
                halves.append(bias[at : at + 1, :] if 0 <= r < WBLK else shut)
            part = raw[kb * BLOCK : (kb + 1) * BLOCK, :] * SCALE2 + jnp.concatenate(halves, axis=1)
            at = first + kb * BLOCK
            if 0 <= at < key_bias.shape[0]:
                col = key_bias[at : at + BLOCK, :]
                part = part + jnp.concatenate([col] * (QROWS // BLOCK), axis=1)
            own = kb - (WBLK - 1)
            if own >= 0:
                part = jnp.where(query_in - key_in >= own * BLOCK, part, NEG)
            parts.append(part)
        parts.append(nt(kg, qb) * SCALE2)
        peak = parts[0].max(axis=0, keepdims=True)
        for part in parts[1:]:
            peak = jnp.maximum(peak, part.max(axis=0, keepdims=True))
        grown = [jnp.exp2(part - peak) for part in parts]
        mass = sum(e.sum(axis=0, keepdims=True) for e in grown)
        inv = 1.0 / mass
        ww = jnp.concatenate([(e * inv).astype(BF) for e in grown], axis=0)
        weights[sb * (N_KEYS + n) : (sb + 1) * (N_KEYS + n), :] = ww
        out_t = tn(vw, ww[0:N_KEYS, :]) + tn(vg, ww[N_KEYS:, :])
        out = out_t.T.astype(BF)
        attn[here, :] = out
        dot = out_t.astype(BF).astype(F32) * d_out[here, :].astype(F32).T
        delta[sb : sb + 1, :] = jnp.sum(dot, axis=0, keepdims=True)


def glob_backward_body(ids, q, d_out, picked, weights, delta, dq_part, dk_glob, dv_glob):
    n = picked.shape[0] // 2
    n_steps = delta.shape[0]
    kg, vg = picked[0:n, :], picked[n:, :]
    dk_glob[...] = jnp.zeros_like(dk_glob)
    dv_glob[...] = jnp.zeros_like(dv_glob)
    for sb in range(n_steps):
        here = slice(sb * QROWS, (sb + 1) * QROWS)
        qb, dob = q[here, :], d_out[here, :]
        wg = weights[sb * (N_KEYS + n) + N_KEYS : (sb + 1) * (N_KEYS + n), :]
        dg = (wg.astype(F32) * (nt(vg, dob) - delta[sb : sb + 1, :])).astype(BF)
        dq_part[sb * HEAD_DIM : (sb + 1) * HEAD_DIM, :] = tn(kg, dg)
        dk_glob[...] += nn(dg, qb)
        dv_glob[...] += nn(wg, dob)


def window_backward_body(steps, n, with_rim, ids, *refs):
    q, d_out, k, v, weights, delta = refs[:6]
    if with_rim:
        rim = refs[6]
        dq_rim, dk, dv, rim_back, dk_rim, dv_rim = refs[-6:]
        for ref in (dk, dv, dk_rim, dv_rim):
            ref[...] = jnp.zeros_like(ref)
    else:
        rim = None
        dq_part, dq_rim = refs[6:8]
        dk, dv, dq = refs[-3:]
        for sb in range(dq_rim.shape[0] // HEAD_DIM):
            here = slice(sb * HEAD_DIM, (sb + 1) * HEAD_DIM)
            dq_t = dq_rim[here, :] + dq_part[here, :]
            dq[sb * QROWS : (sb + 1) * QROWS, :] = (dq_t.T * SCALE).astype(BF)
    for sb in steps:
        here = slice(sb * QROWS, (sb + 1) * QROWS)
        _, cut, inner, kw, vw = window_keys(sb, k, v, rim)
        qb, dob = q[here, :], d_out[here, :]
        at = sb * (N_KEYS + n)
        ww = weights[at : at + N_KEYS, :]
        dw = (ww.astype(F32) * (nt(vw, dob) - delta[sb : sb + 1, :])).astype(BF)
        part = slice(sb * HEAD_DIM, (sb + 1) * HEAD_DIM)
        if with_rim:
            dq_rim[part, :] = tn(kw, dw)
        else:
            dq_t = tn(kw, dw) + dq_part[part, :]
            dq[here, :] = (dq_t.T * SCALE).astype(BF)
        dkw, dvw = nn(dw, qb), nn(ww, dob)
        if cut:
            dk_rim[RIM - cut :, :] += dkw[0:cut, :]
            dv_rim[RIM - cut :, :] += dvw[0:cut, :]
        dk[inner, :] += dkw[cut:, :]
        dv[inner, :] += dvw[cut:, :]
    if with_rim:
        rim_back[0:RIM, :] = dk_rim[...].astype(BF)
        rim_back[RIM:, :] = dv_rim[...].astype(BF)


def row_backward_body(ids, picked, k, v, mine, other, dkg, dvg, dk, dv, sums):
    n = picked.shape[0] // 2
    step = 512
    query, d_out = picked[0:n, :], picked[n:, :]
    peak, mass, dot, _, _ = merged(mine, other)
    lse = peak + jnp.log2(mass)
    delta = dot / mass
    dq_t = jnp.zeros((HEAD_DIM, n), F32)
    for c in range(0, k.shape[0], step):
        keys, vals = k[c : c + step, :], v[c : c + step, :]
        prob = jnp.exp2(nt(keys, query) * SCALE2 - lse)
        ds = (prob * (nt(vals, d_out) - delta)).astype(BF)
        dk[c : c + step, :] = nn(ds, query)
        dv[c : c + step, :] = nn(prob.astype(BF), d_out)
        dq_t = dq_t + tn(keys, ds)
    sums[0:n, :] = (dq_t.T * SCALE).astype(BF)
    sums[n : 2 * n, :] = dkg[...].astype(BF)
    sums[2 * n :, :] = dvg[...].astype(BF)


def pack_rows_body(ids, pos_row, attn, mine, other, *refs):
    outs, attn_f = refs[:-1], refs[-1]
    tok = attn.shape[0] // len(outs)
    attn_f[...] = attn[...]

    @pl.when(ids[1] == 0)
    def _():
        _, _, _, wa, wb = merged(mine, other)
        both_t = merged_attn(mine, other, wa, wb)
        hit = place_rows(pos_row[...], tok)
        is_row = jnp.max(hit.astype(F32), axis=1, keepdims=True) > 0.5
        placed = nt(hit.astype(BF), both_t)
        attn_f[0:tok, :] = jnp.where(is_row, placed, attn[0:tok, :].astype(F32)).astype(BF)

    for i, out in enumerate(outs):
        out[...] = attn_f[rows(ids[0] ^ i, tok), :]


def project_body(ids, w, *refs):
    pieces, (keep, send, attn) = refs[:-3], refs[-3:]
    for i, piece in enumerate(pieces):
        attn[:, rows(ids[0] ^ i, HEAD_DIM)] = piece[...]
    cols = keep.shape[2]
    a = attn[...]
    me = ids[2]
    for i, group in enumerate((me, me ^ 2)):
        keep[i] = nn(a, w[:, rows(group, cols)]).astype(BF)
    for i, group in enumerate((me ^ 1, me ^ 3)):
        send[i] = nn(a, w[:, rows(group, cols)]).astype(BF)


def pack_grads_body(ids, pos_row, dq, dk, dv, rk, rv, rim_back, sums, other, *refs):
    outs, (dqf, dkf, dvf) = refs[:-3], refs[-3:]
    total = dk.shape[0]
    tok = total // len(outs)
    n = sums.shape[0] // 3
    dqf[...] = dq[...]
    dkf[...] = dk[...] + rk[...]
    dvf[...] = dv[...] + rv[...]
    dkf[total - RIM :, :] += rim_back[0:RIM, :].astype(F32)
    dvf[total - RIM :, :] += rim_back[RIM:, :].astype(F32)

    @pl.when(ids[1] == 0)
    def _():
        both = (sums[...].astype(F32) + other[...].astype(F32)).astype(BF)
        hit = place_rows(pos_row[...], tok).astype(BF)
        dqf[0:tok, :] = (dqf[0:tok, :].astype(F32) + nn(hit, both[0:n, :])).astype(BF)
        dkf[0:tok, :] += nn(hit, both[n : 2 * n, :])
        dvf[0:tok, :] += nn(hit, both[2 * n :, :])

    for i, out in enumerate(outs):
        here = rows(ids[0] ^ i, tok)
        out[0:tok, :] = dqf[here, :]
        out[tok : 2 * tok, :] = (dkf[here, :] * SCALE).astype(BF)
        out[2 * tok :, :] = dvf[here, :].astype(BF)


def join_grads_body(ids, *refs):
    pieces, outs = refs[:-3], refs[-3:]
    tok = outs[0].shape[0]
    for i, piece in enumerate(pieces):
        col = rows(ids[0] ^ i, HEAD_DIM)
        for at, out in enumerate(outs):
            out[:, col] = piece[at * tok : (at + 1) * tok, :]


def on_device(queries, keys, values, out_weight, out_grad, global_pos, block_mask):
    tok, cols = queries.shape
    heads = cols // HEAD_DIM
    n_seq = lax.axis_size("seq")
    n_groups = n_seq // heads
    total = heads * tok
    n_glob = global_pos.shape[0]
    seq_index = lax.axis_index("seq")
    group = seq_index // heads
    ids = jnp.stack([seq_index % heads, group, lax.axis_index("head")]).astype(jnp.int32)
    pos_col = global_pos.reshape(n_glob, 1)
    pos_row = global_pos.reshape(1, n_glob)

    def swap_in_group(pieces):
        moved = [
            lax.ppermute(piece, "seq", [(s, s ^ i) for s in range(n_seq)])
            for i, piece in enumerate(pieces)
            if i
        ]
        return [pieces[0]] + moved

    def from_first(x):
        d = 1
        while d < n_groups:
            route = [
                (g * heads + j, (g + d) * heads + j)
                for g in range(d)
                for j in range(heads)
                if g + d < n_groups
            ]
            x = jnp.where((group >= d) & (group < 2 * d), lax.ppermute(x, "seq", route), x)
            d *= 2
        return x

    def to_next_group(x, step):
        route = [(s, s + step * heads) for s in range(n_seq) if 0 <= s + step * heads < n_seq]
        return lax.ppermute(x, "seq", route)

    def with_group(x, d):
        return lax.ppermute(x, "seq", [(s, s ^ (d * heads)) for s in range(n_seq)])

    kv_packed = local_call(
        "pack_kv",
        pack_kv_body,
        ids,
        (),
        [((2 * tok, HEAD_DIM), BF)] * heads,
        [pltpu.SemaphoreType.DMA((2 * heads,))],
        far=((keys, pltpu.HBM), (values, pltpu.HBM)),
        mib=PACK_MIB,
        out_space=pltpu.VMEM,
    )
    kv = swap_in_group(kv_packed)
    qo = swap_in_group(
        local_call(
            "pack_qo",
            pack_qo_body,
            ids,
            (queries, out_grad, out_weight),
            [((2 * tok + block_mask.size, HEAD_DIM), BF)] * heads,
            [pltpu.VMEM((tok, cols), BF)],
            far=((block_mask, pltpu.SMEM),),
            after=(kv_packed[0],),
        )
    )
    head_rows = ((total, HEAD_DIM), BF)
    head_sums = ((total, HEAD_DIM), F32)
    glob_sums = ((n_glob, HEAD_DIM), F32)
    k, v, key_bias, picked, rim_out = local_call(
        "join_kv",
        join_kv_body,
        ids,
        (pos_col, pos_row, *kv),
        [
            head_rows,
            head_rows,
            ((tok, HEAD_DIM), F32),
            ((2 * n_glob, HEAD_DIM), BF),
            ((2 * RIM, HEAD_DIM), BF),
        ],
    )
    kv_glob = from_first(picked)
    rim = to_next_group(rim_out, 1)
    q, d_attn, bias, qo_pick = local_call(
        "join_qo",
        join_qo_body,
        ids,
        (pos_col, pos_row, *qo),
        [
            head_rows,
            head_rows,
            ((heads * block_mask.size, HEAD_DIM), F32),
            ((2 * n_glob, HEAD_DIM), BF),
        ],
        after=(picked,),
    )
    qo_glob = from_first(qo_pick)
    n_steps = total // QROWS
    base = (q, d_attn, k, v, kv_glob)
    forward_types = [
        head_rows,
        ((n_steps * (N_KEYS + n_glob), QROWS), BF),
        ((n_steps, QROWS), F32),
    ]
    backward_types = [head_rows, head_sums, head_sums, glob_sums, glob_sums]
    rim_type = [((2 * RIM, HEAD_DIM), BF)]

    def window(name, body, args, state, outs, scratch=(), after=()):
        at = 1 + len(args)
        return local_call(
            name,
            body,
            ids,
            tuple(args) + tuple(state),
            outs,
            scratch,
            after=after,
            aliases={at + i: i for i in range(len(state))},
            mib=20,
        )

    seen = window(
        "forward_inner",
        functools.partial(window_forward_body, range(2, n_steps), False),
        base + (bias, key_bias),
        (),
        forward_types,
    )
    attn, weights, delta = window(
        "forward_rim",
        functools.partial(window_forward_body, range(0, 2), True),
        base + (bias, key_bias, rim),
        seen,
        forward_types,
    )
    backward = (q, d_attn, k, v, weights, delta)
    dq_rim, *state, rim_sum = window(
        "backward_rim",
        functools.partial(window_backward_body, range(0, 2), n_glob, True),
        backward + (rim,),
        (),
        [((2 * HEAD_DIM, QROWS), F32), head_sums, head_sums, ((2 * RIM, HEAD_DIM), BF)],
        [pltpu.VMEM((RIM, HEAD_DIM), F32)] * 2,
    )
    rim_back = to_next_group(rim_sum, -1)
    packed_rows = ((HEAD_DIM + 16, n_glob), BF)
    mine = local_call(
        "row_forward",
        row_forward_body,
        ids,
        (qo_glob, k, v),
        [packed_rows],
        [pltpu.VMEM((total, n_glob), F32)],
        after=(rim_sum,),
    )[0]
    d = 1
    while 2 * d < n_groups:
        mine = local_call("merge", merge_body, ids, (mine, with_group(mine, d)), [packed_rows])[0]
        d *= 2
    other = with_group(mine, d)
    dq_part, dkg, dvg = local_call(
        "glob_backward",
        glob_backward_body,
        ids,
        (q, d_attn, kv_glob, weights, delta),
        [((n_steps * HEAD_DIM, QROWS), F32), glob_sums, glob_sums],
        after=(mine,),
    )
    rk, rv, sums = local_call(
        "row_backward",
        row_backward_body,
        ids,
        (qo_glob, k, v, mine, other, dkg, dvg),
        [head_sums, head_sums, ((3 * n_glob, HEAD_DIM), BF)],
    )
    attn_parts = swap_in_group(
        local_call(
            "pack_rows",
            pack_rows_body,
            ids,
            (pos_row, attn, mine, other),
            [((tok, HEAD_DIM), BF)] * heads,
            [pltpu.VMEM((total, HEAD_DIM), BF)],
            after=(sums,),
        )
    )
    dk, dv, dq = window(
        "backward_inner",
        functools.partial(window_backward_body, range(2, n_steps), n_glob, False),
        backward + (dq_part, dq_rim),
        state,
        [head_sums, head_sums, head_rows],
        after=(attn_parts[0],),
    )

    def to_lower(x, d):
        route = [
            (g * heads + j, (g - d) * heads + j)
            for g in range(d, min(2 * d, n_groups))
            for j in range(heads)
        ]
        return lax.ppermute(x, "seq", route)

    d = n_groups // 2
    while d > 1:
        sums = (sums.astype(F32) + to_lower(sums, d).astype(F32)).astype(BF)
        d //= 2
    other_sums = to_lower(sums, 1)
    grads = swap_in_group(
        local_call(
            "pack_grads",
            pack_grads_body,
            ids,
            (pos_row, dq, dk, dv, rk, rv, rim_back, sums, other_sums),
            [((3 * tok, HEAD_DIM), BF)] * heads,
            [
                pltpu.VMEM((total, HEAD_DIM), BF),
                pltpu.VMEM((total, HEAD_DIM), F32),
                pltpu.VMEM((total, HEAD_DIM), F32),
            ],
        )
    )
    n_head = lax.axis_size("head")
    out_cols = out_weight.shape[1] // n_head
    keep, send = local_call(
        "project",
        project_body,
        ids,
        (out_weight, *attn_parts),
        [((2, tok, out_cols), BF)] * 2,
        [pltpu.VMEM((tok, cols), BF)],
        after=(grads[0],),
    )
    half = lax.ppermute(send, "head", [(h, h ^ 1) for h in range(n_head)])
    summed = keep.astype(F32) + half.astype(F32)
    far = lax.ppermute(summed[1].astype(BF), "head", [(h, h ^ 2) for h in range(n_head)])
    layer_out = (summed[0] + far.astype(F32)).astype(BF)
    grad_queries, grad_keys, grad_values = local_call(
        "join_grads", join_grads_body, ids, tuple(grads), [((tok, cols), BF)] * 3, us=JOIN_US
    )
    return (layer_out, grad_queries, grad_keys, grad_values)


def solution(mesh):
    return jax.shard_map(
        on_device,
        mesh=mesh,
        in_specs=(
            P("seq", "head"),
            P("seq", "head"),
            P("seq", "head"),
            P("head", None),
            P("seq", None),
            P(),
            P("seq", None),
        ),
        out_specs=(P("seq", "head"), P("seq", "head"), P("seq", "head"), P("seq", "head")),
        check_vma=False,
    )
```

```python
import functools
import math

import jax
import jax.numpy as jnp
from jax import lax
from jax.experimental import pallas as pl
from jax.experimental.pallas import tpu as pltpu
from jax.sharding import PartitionSpec as P

HEAD_DIM = 128
BLOCK = 128
WBLK = 4
RIM = (WBLK - 1) * BLOCK
QROWS = 2 * BLOCK
SCALE = 1.0 / math.sqrt(HEAD_DIM)
SCALE2 = SCALE * math.log2(math.e)
BF = jnp.bfloat16
F32 = jnp.float32
NEG = float("-inf")
FLOOR = -1e30
JOIN_US = 12.0
PACK_MIB = 14


def nn(a, b):
    return lax.dot_general(a, b, (((1,), (0,)), ((), ())), preferred_element_type=F32)


def nt(a, b):
    return lax.dot_general(a, b, (((1,), (1,)), ((), ())), preferred_element_type=F32)


def rows(slot, count):
    return pl.ds(pl.multiple_of(slot * count, count), count)


def local_call(name, body, ids, arrays, outs, scratch=(), after=(), aliases=None, far=(), mib=14, us=0.0, out_space=pltpu.VMEM):
    first = 1 + len(arrays) + len(far)

    def kernel(*refs):
        body(*refs[:first], *refs[first + len(after) :])

    return pl.pallas_call(
        kernel,
        name=name,
        out_shape=tuple(jax.ShapeDtypeStruct(s, t) for s, t in outs),
        in_specs=[pl.BlockSpec(memory_space=pltpu.SMEM)]
        + [pl.BlockSpec(memory_space=pltpu.VMEM)] * len(arrays)
        + [pl.BlockSpec(memory_space=space) for _, space in far]
        + [pl.BlockSpec(memory_space=pl.ANY)] * len(after),
        out_specs=tuple(pl.BlockSpec(memory_space=out_space) for _ in outs),
        scratch_shapes=list(scratch),
        compiler_params=pltpu.CompilerParams(vmem_limit_bytes=mib * 2**20),
        input_output_aliases=aliases or {},
        cost_estimate=pl.CostEstimate(
            flops=1000 + int(us * 1.15e9), bytes_accessed=1000, transcendentals=0
        ),
    )(ids, *arrays, *[array for array, _ in far], *after)


def pack_kv_body(ids, k, v, *refs):
    outs, sems = refs[:-1], refs[-1]
    tok = k.shape[0]
    copies = []
    for i, out in enumerate(outs):
        col = rows(ids[0] ^ i, HEAD_DIM)
        copies += [
            pltpu.make_async_copy(k.at[:, col], out.at[0:tok, :], sems.at[2 * i]),
            pltpu.make_async_copy(v.at[:, col], out.at[tok:, :], sems.at[2 * i + 1]),
        ]
    for copy in copies:
        copy.start()
    for copy in copies:
        copy.wait()


def pack_qo_body(ids, q, out_grad, out_weight, block_mask, *refs):
    outs, d_attn = refs[:-1], refs[-1]
    tok = q.shape[0]
    entries = outs[0].shape[0] - 2 * tok
    at = lax.broadcasted_iota(jnp.int32, (entries, HEAD_DIM), 0)
    mask = jnp.zeros((entries, HEAD_DIM), jnp.int32)
    for e in range(entries):
        mask = jnp.where(at == e, block_mask[e // WBLK, e % WBLK], mask)
    mask = mask.astype(F32).astype(BF)
    d_attn[...] = nt(out_grad[...], out_weight[...]).astype(BF)
    for i, out in enumerate(outs):
        col = rows(ids[0] ^ i, HEAD_DIM)
        out[0:tok, :] = q[:, col]
        out[tok : 2 * tok, :] = d_attn[:, col]
        out[2 * tok :, :] = mask


def pick_rows(pos_col, tok):
    hits = pos_col == lax.broadcasted_iota(jnp.int32, (pos_col.shape[0], tok), 1)
    return hits.astype(BF)


def place_rows(pos_row, tok):
    return lax.broadcasted_iota(jnp.int32, (tok, pos_row.shape[1]), 0) == pos_row


def row_column(pos_row, tok):
    hit = place_rows(pos_row, tok).astype(F32)
    return jnp.max(hit, axis=1, keepdims=True) > 0.5


def join_kv_body(ids, pos_col, pos_row, *refs):
    pieces, (k, v, key_bias, picked, rim) = refs[:-5], refs[-5:]
    tok = k.shape[0] // len(pieces)
    for i, piece in enumerate(pieces):
        slot = ids[0] ^ i
        k[rows(slot, tok), :] = piece[0:tok, :]
        v[rows(slot, tok), :] = piece[tok:, :]
    picks = pick_rows(pos_col[...], tok)
    n = pos_col.shape[0]
    picked[0:n, :] = nn(picks, k[0:tok, :]).astype(BF)
    picked[n:, :] = nn(picks, v[0:tok, :]).astype(BF)
    rim[0:RIM, :] = k[k.shape[0] - RIM :, :]
    rim[RIM:, :] = v[k.shape[0] - RIM :, :]
    hidden = jnp.logical_and(row_column(pos_row[...], tok), ids[1] == 0)
    key_bias[...] = jnp.where(hidden, NEG, jnp.zeros(key_bias.shape, F32))


def turn_body(ids, k, v, kt, vt):
    kt[...] = k[...].T
    vt[...] = v[...].T


def join_qo_body(ids, pos_col, pos_row, *refs):
    pieces, (q, d_attn, bias, picked) = refs[:-4], refs[-4:]
    tok = q.shape[0] // len(pieces)
    n_rows = bias.shape[0] // len(pieces)
    n = pos_col.shape[0]
    for i, piece in enumerate(pieces):
        slot = ids[0] ^ i
        q[rows(slot, tok), :] = piece[0:tok, :]
        d_attn[rows(slot, tok), :] = piece[tok : 2 * tok, :]
        open_ = piece[2 * tok :, :].astype(F32)
        entry = lax.broadcasted_iota(jnp.int32, open_.shape, 0) + slot * n_rows
        inside = (ids[1] > 0) | (entry // WBLK >= entry % WBLK)
        bias[rows(slot, n_rows), :] = jnp.where((open_ > 0.5) & inside, 0.0, NEG)

    @pl.when(ids[1] == 0)
    def _():
        picks = pick_rows(pos_col[...], tok)
        picked[0:n, :] = nn(picks, q[0:tok, :]).astype(BF)
        picked[n:, :] = nn(picks, d_attn[0:tok, :]).astype(BF)
        is_row = row_column(pos_row[...], tok)
        kept = jnp.where(is_row, 0.0, d_attn[0:tok, :].astype(F32))
        d_attn[0:tok, :] = kept.astype(BF)

    @pl.when(ids[1] > 0)
    def _():
        picked[...] = jnp.zeros_like(picked)


def row_forward_body(ids, own, sent, k, v, vt, mine, scores):
    picked = ours(ids, own, sent)
    n = picked.shape[0] // 2
    step = 512
    query, d_out = picked[0:n, :], picked[n:, :]
    peak = None
    for c in range(0, k.shape[0], step):
        s = nt(k[c : c + step, :], query) * SCALE2
        scores[c : c + step, :] = s
        top = jnp.max(s, axis=0, keepdims=True)
        peak = top if peak is None else jnp.maximum(peak, top)
    mass = jnp.zeros((1, n), F32)
    dot = jnp.zeros((1, n), F32)
    numer = jnp.zeros((HEAD_DIM, n), F32)
    for c in range(0, k.shape[0], step):
        e = jnp.exp2(scores[c : c + step, :] - peak)
        vals = v[c : c + step, :]
        mass = mass + jnp.sum(e, axis=0, keepdims=True)
        dot = dot + jnp.sum(e * nt(vals, d_out), axis=0, keepdims=True)
        numer = numer + nn(vt[:, c : c + step], e.astype(BF))
    mine[0:HEAD_DIM, :] = (numer / mass).astype(BF)
    mine[HEAD_DIM:, :] = in_thirds((peak, mass, dot))


def in_thirds(values):
    parts = []
    for value in values:
        for _ in range(3):
            part = value.astype(BF).astype(F32)
            parts.append(part)
            value = value - part
    empty = jnp.zeros((16 - len(parts), parts[0].shape[1]), F32)
    return jnp.concatenate(parts + [empty], axis=0).astype(BF)


def merged(mine, other):
    thirds = [ref[HEAD_DIM:, :].astype(F32) for ref in (mine, other)]
    (pa, ma, da), (pb, mb, db) = [
        [t[3 * i : 3 * i + 1] + t[3 * i + 1 : 3 * i + 2] + t[3 * i + 2 : 3 * i + 3] for i in range(3)]
        for t in thirds
    ]
    peak = jnp.maximum(pa, pb)
    wa, wb = jnp.exp2(pa - peak), jnp.exp2(pb - peak)
    mass = ma * wa + mb * wb
    return peak, mass, da * wa + db * wb, ma * wa / mass, mb * wb / mass


def merged_attn(mine, other, wa, wb):
    both = mine[0:HEAD_DIM, :].astype(F32) * wa + other[0:HEAD_DIM, :].astype(F32) * wb
    return both.astype(BF)


def merge_body(ids, mine, other, out):
    peak, mass, dot, wa, wb = merged(mine, other)
    out[0:HEAD_DIM, :] = merged_attn(mine, other, wa, wb)
    out[HEAD_DIM:, :] = in_thirds((peak, mass, dot))


N_KEYS = RIM + QROWS


def window_span(sb):
    first = sb * QROWS - RIM
    cut = max(0, -first)
    return first, cut, slice(first + cut, (sb + 1) * QROWS)


def window_rows(sb, own, rim):
    _, cut, inner = window_span(sb)
    if not cut:
        return own[inner, :]
    return jnp.concatenate([rim[RIM - cut : RIM, :], own[inner, :]], axis=0)


def window_cols(sb, own_t, rim):
    _, cut, inner = window_span(sb)
    if not cut:
        return own_t[:, inner]
    return jnp.concatenate([rim[RIM - cut : RIM, :].T, own_t[:, inner]], axis=1)


def window_forward_body(steps, with_rim, ids, *refs):
    q, k, vt, bias, key_bias = refs[:5]
    k_rim, v_rim = (refs[5].at[0:RIM], refs[5].at[RIM:]) if with_rim else (None, None)
    weights, out_t, peaks, masses = refs[-4:]
    key_in = lax.broadcasted_iota(jnp.int32, (BLOCK, QROWS), 0)
    query_in = lax.broadcasted_iota(jnp.int32, (BLOCK, QROWS), 1)
    shut = jnp.full((1, BLOCK), NEG, F32)
    for sb in steps:
        here = slice(sb * QROWS, (sb + 1) * QROWS)
        first = window_span(sb)[0]
        kw, vwt = window_rows(sb, k, k_rim), window_cols(sb, vt, v_rim)
        raw = nt(kw, q[here, :])
        parts = []
        for kb in range(N_KEYS // BLOCK):
            halves = []
            for half in range(QROWS // BLOCK):
                r = half + WBLK - 1 - kb
                at = (sb * (QROWS // BLOCK) + half) * WBLK + r
                halves.append(bias[at : at + 1, :] if 0 <= r < WBLK else shut)
            part = raw[kb * BLOCK : (kb + 1) * BLOCK, :] * SCALE2 + jnp.concatenate(halves, axis=1)
            at = first + kb * BLOCK
            if 0 <= at < key_bias.shape[0]:
                col = key_bias[at : at + BLOCK, :]
                part = part + jnp.concatenate([col] * (QROWS // BLOCK), axis=1)
            own = kb - (WBLK - 1)
            if own >= 0:
                part = jnp.where(query_in - key_in >= own * BLOCK, part, NEG)
            parts.append(part)
        peak = jnp.full((1, QROWS), FLOOR, F32)
        for part in parts:
            peak = jnp.maximum(peak, part.max(axis=0, keepdims=True))
        grown = [jnp.exp2(part - peak) for part in parts]
        masses[sb : sb + 1, :] = sum(e.sum(axis=0, keepdims=True) for e in grown)
        peaks[sb : sb + 1, :] = peak
        ww = jnp.concatenate([e.astype(BF) for e in grown], axis=0)
        weights[sb * N_KEYS : (sb + 1) * N_KEYS, :] = ww
        out_t[sb * HEAD_DIM : (sb + 1) * HEAD_DIM, :] = nn(vwt, ww)


def ours(ids, mine, sent):
    return jnp.where(ids[1] < ids[3], mine[...], sent[...])


def glob_forward_body(ids, q, d_out, picked, out_t, peaks, masses, *refs):
    attn, weights, d_win, d_glob, delta_win, delta_glob = refs
    n = picked.shape[0] // 2
    kg, vgt = picked[0:n, :], picked[n:, :].T
    for sb in range(peaks.shape[0]):
        here = slice(sb * QROWS, (sb + 1) * QROWS)
        row = slice(sb, sb + 1)
        score = nt(kg, q[here, :]) * SCALE2
        peak = jnp.maximum(peaks[row, :], score.max(axis=0, keepdims=True))
        grown = jnp.exp2(score - peak)
        part = jnp.exp2(peaks[row, :] - peak)
        inv = 1.0 / (masses[row, :] * part + grown.sum(axis=0, keepdims=True))
        part = part * inv
        wg = grown.astype(BF)
        weights[sb * n : (sb + 1) * n, :] = wg
        both = out_t[sb * HEAD_DIM : (sb + 1) * HEAD_DIM, :] * part + nn(vgt, wg) * inv
        attn[here, :] = both.T.astype(BF)
        d_t = d_out[here, :].astype(F32).T
        delta = jnp.sum(both.astype(BF).astype(F32) * d_t, axis=0, keepdims=True)
        d_win[here, :] = (d_t * part).T.astype(BF)
        d_glob[here, :] = (d_t * inv).T.astype(BF)
        delta_win[row, :] = delta * part
        delta_glob[row, :] = delta * inv


def glob_backward_body(ids, q, d_out, picked, weights, delta, dq_part, dk_glob, dv_glob):
    n = picked.shape[0] // 2
    n_steps = delta.shape[0]
    kt, vg = picked[0:n, :].T, picked[n:, :]
    wide = 2
    dkg = jnp.zeros(dk_glob.shape, F32)
    dvg = jnp.zeros(dv_glob.shape, F32)
    for c in range(0, n_steps, wide):
        here = slice(c * QROWS, (c + wide) * QROWS)
        qb, dob = q[here, :], d_out[here, :]
        wg = jnp.concatenate(
            [weights[sb * n : (sb + 1) * n, :] for sb in range(c, c + wide)], axis=1
        )
        off = jnp.concatenate([delta[sb : sb + 1, :] for sb in range(c, c + wide)], axis=1)
        dg = (wg.astype(F32) * (nt(vg, dob) - off)).astype(BF)
        dq_t = nn(kt, dg)
        for i in range(wide):
            dq_part[(c + i) * HEAD_DIM : (c + i + 1) * HEAD_DIM, :] = dq_t[:, i * QROWS : (i + 1) * QROWS]
        dkg = dkg + nn(dg, qb)
        dvg = dvg + nn(wg, dob)
    dk_glob[...] = dkg
    dv_glob[...] = dvg


def window_backward_body(steps, with_rim, ids, *refs):
    q, d_out, kt, v, weights, delta = refs[:6]
    k_rim, v_rim = (refs[6].at[0:RIM], refs[6].at[RIM:]) if with_rim else (None, None)
    if with_rim:
        dq_rim, dk, dv, rim_back, dk_rim, dv_rim = refs[-6:]
        for ref in (dk, dv, dk_rim, dv_rim):
            ref[...] = jnp.zeros_like(ref)
    else:
        dq_part, dq_rim = refs[6:8]
        dk, dv, dq = refs[-3:]
        for sb in range(dq_rim.shape[0] // HEAD_DIM):
            here = slice(sb * HEAD_DIM, (sb + 1) * HEAD_DIM)
            dq_t = dq_rim[here, :] + dq_part[here, :]
            dq[sb * QROWS : (sb + 1) * QROWS, :] = (dq_t.T * SCALE).astype(BF)
    for sb in steps:
        here = slice(sb * QROWS, (sb + 1) * QROWS)
        _, cut, inner = window_span(sb)
        kwt, vw = window_cols(sb, kt, k_rim), window_rows(sb, v, v_rim)
        qb, dob = q[here, :], d_out[here, :]
        ww = weights[sb * N_KEYS : (sb + 1) * N_KEYS, :]
        dw = (ww.astype(F32) * (nt(vw, dob) - delta[sb : sb + 1, :])).astype(BF)
        part = slice(sb * HEAD_DIM, (sb + 1) * HEAD_DIM)
        if with_rim:
            dq_rim[part, :] = nn(kwt, dw)
        else:
            dq_t = nn(kwt, dw) + dq_part[part, :]
            dq[here, :] = (dq_t.T * SCALE).astype(BF)
        dkw, dvw = nn(dw, qb), nn(ww, dob)
        if cut:
            dk_rim[RIM - cut :, :] += dkw[0:cut, :]
            dv_rim[RIM - cut :, :] += dvw[0:cut, :]
        dk[inner, :] += dkw[cut:, :]
        dv[inner, :] += dvw[cut:, :]
    if with_rim:
        rim_back[0:RIM, :] = dk_rim[...].astype(BF)
        rim_back[RIM:, :] = dv_rim[...].astype(BF)


def row_backward_body(ids, own, sent, k, v, kt, mine, other, dkg, dvg, dk, dv, sums):
    picked = ours(ids, own, sent)
    n = picked.shape[0] // 2
    step = 512
    query, d_out = picked[0:n, :], picked[n:, :]
    peak, mass, dot, _, _ = merged(mine, other)
    lse = peak + jnp.log2(mass)
    delta = dot / mass
    dq_t = jnp.zeros((HEAD_DIM, n), F32)
    for c in range(0, k.shape[0], step):
        keys, vals = k[c : c + step, :], v[c : c + step, :]
        prob = jnp.exp2(nt(keys, query) * SCALE2 - lse)
        ds = (prob * (nt(vals, d_out) - delta)).astype(BF)
        dk[c : c + step, :] = nn(ds, query)
        dv[c : c + step, :] = nn(prob.astype(BF), d_out)
        dq_t = dq_t + nn(kt[:, c : c + step], ds)
    sums[0:n, :] = (dq_t.T * SCALE).astype(BF)
    sums[n : 2 * n, :] = dkg[...].astype(BF)
    sums[2 * n :, :] = dvg[...].astype(BF)


def pack_rows_body(ids, pos_row, attn, mine, other, *refs):
    outs, attn_f = refs[:-1], refs[-1]
    tok = attn.shape[0] // len(outs)
    attn_f[...] = attn[...]

    @pl.when(ids[1] == 0)
    def _():
        _, _, _, wa, wb = merged(mine, other)
        both_t = merged_attn(mine, other, wa, wb)
        hit = place_rows(pos_row[...], tok)
        is_row = jnp.max(hit.astype(F32), axis=1, keepdims=True) > 0.5
        placed = nt(hit.astype(BF), both_t)
        attn_f[0:tok, :] = jnp.where(is_row, placed, attn[0:tok, :].astype(F32)).astype(BF)

    for i, out in enumerate(outs):
        out[...] = attn_f[rows(ids[0] ^ i, tok), :]


def project_body(ids, w, *refs):
    pieces, (keep, send, attn) = refs[:-3], refs[-3:]
    for i, piece in enumerate(pieces):
        attn[:, rows(ids[0] ^ i, HEAD_DIM)] = piece[...]
    cols = keep.shape[2]
    a = attn[...]
    me = ids[2]
    for i, group in enumerate((me, me ^ 2)):
        keep[i] = nn(a, w[:, rows(group, cols)]).astype(BF)
    for i, group in enumerate((me ^ 1, me ^ 3)):
        send[i] = nn(a, w[:, rows(group, cols)]).astype(BF)


def pack_grads_body(ids, pos_row, dq, dk, dv, rk, rv, rim_back, sums, other, *refs):
    outs, (dqf, dkf, dvf) = refs[:-3], refs[-3:]
    total = dk.shape[0]
    tok = total // len(outs)
    n = sums.shape[0] // 3
    dqf[...] = dq[...]
    dkf[...] = dk[...] + rk[...]
    dvf[...] = dv[...] + rv[...]
    dkf[total - RIM :, :] += rim_back[0:RIM, :].astype(F32)
    dvf[total - RIM :, :] += rim_back[RIM:, :].astype(F32)

    @pl.when(ids[1] == 0)
    def _():
        both = (sums[...].astype(F32) + other[...].astype(F32)).astype(BF)
        hit = place_rows(pos_row[...], tok).astype(BF)
        dqf[0:tok, :] = (dqf[0:tok, :].astype(F32) + nn(hit, both[0:n, :])).astype(BF)
        dkf[0:tok, :] += nn(hit, both[n : 2 * n, :])
        dvf[0:tok, :] += nn(hit, both[2 * n :, :])

    for i, out in enumerate(outs):
        here = rows(ids[0] ^ i, tok)
        out[0:tok, :] = dqf[here, :]
        out[tok : 2 * tok, :] = (dkf[here, :] * SCALE).astype(BF)
        out[2 * tok :, :] = dvf[here, :].astype(BF)


def join_grads_body(ids, *refs):
    pieces, outs = refs[:-3], refs[-3:]
    tok = outs[0].shape[0]
    for i, piece in enumerate(pieces):
        col = rows(ids[0] ^ i, HEAD_DIM)
        for at, out in enumerate(outs):
            out[:, col] = piece[at * tok : (at + 1) * tok, :]


def on_device(queries, keys, values, out_weight, out_grad, global_pos, block_mask):
    tok, cols = queries.shape
    heads = cols // HEAD_DIM
    n_seq = lax.axis_size("seq")
    n_groups = n_seq // heads
    total = heads * tok
    n_glob = global_pos.shape[0]
    seq_index = lax.axis_index("seq")
    group = seq_index // heads
    last = 1
    while 2 * last < n_groups:
        last *= 2
    ids = jnp.stack([seq_index % heads, group, lax.axis_index("head"), jnp.int32(last)])
    ids = ids.astype(jnp.int32)
    pos_col = global_pos.reshape(n_glob, 1)
    pos_row = global_pos.reshape(1, n_glob)

    def swap_in_group(pieces):
        moved = [
            lax.ppermute(piece, "seq", [(s, s ^ i) for s in range(n_seq)])
            for i, piece in enumerate(pieces)
            if i
        ]
        return [pieces[0]] + moved

    def from_first(x):
        d = 1
        while True:
            route = [
                (g * heads + j, (g + d) * heads + j)
                for g in range(d)
                for j in range(heads)
                if g + d < n_groups
            ]
            sent = lax.ppermute(x, "seq", route)
            if 2 * d >= n_groups:
                return x, sent
            x = jnp.where((group >= d) & (group < 2 * d), sent, x)
            d *= 2

    def to_next_group(x, step):
        route = [(s, s + step * heads) for s in range(n_seq) if 0 <= s + step * heads < n_seq]
        return lax.ppermute(x, "seq", route)

    def with_group(x, d):
        return lax.ppermute(x, "seq", [(s, s ^ (d * heads)) for s in range(n_seq)])

    kv_packed = local_call(
        "pack_kv",
        pack_kv_body,
        ids,
        (),
        [((2 * tok, HEAD_DIM), BF)] * heads,
        [pltpu.SemaphoreType.DMA((2 * heads,))],
        far=((keys, pltpu.HBM), (values, pltpu.HBM)),
        mib=PACK_MIB,
        out_space=pltpu.VMEM,
    )
    kv = swap_in_group(kv_packed)
    qo = swap_in_group(
        local_call(
            "pack_qo",
            pack_qo_body,
            ids,
            (queries, out_grad, out_weight),
            [((2 * tok + block_mask.size, HEAD_DIM), BF)] * heads,
            [pltpu.VMEM((tok, cols), BF)],
            far=((block_mask, pltpu.SMEM),),
            after=(kv_packed[0],),
        )
    )
    head_rows = ((total, HEAD_DIM), BF)
    head_sums = ((total, HEAD_DIM), F32)
    glob_sums = ((n_glob, HEAD_DIM), F32)
    k, v, key_bias, picked, rim_out = local_call(
        "join_kv",
        join_kv_body,
        ids,
        (pos_col, pos_row, *kv),
        [
            head_rows,
            head_rows,
            ((tok, HEAD_DIM), F32),
            ((2 * n_glob, HEAD_DIM), BF),
            ((2 * RIM, HEAD_DIM), BF),
        ],
    )
    kv_own, kv_sent = from_first(picked)
    kv_glob = jnp.where(group >= last, kv_sent, kv_own)
    kt, vt = local_call("turn", turn_body, ids, (k, v), [((HEAD_DIM, total), BF)] * 2)
    rim_out, qo[2] = lax.optimization_barrier((rim_out, qo[2]))
    rim = to_next_group(rim_out, 1)
    q, d_attn, bias, qo_pick = local_call(
        "join_qo",
        join_qo_body,
        ids,
        (pos_col, pos_row, *qo),
        [
            head_rows,
            head_rows,
            ((heads * block_mask.size, HEAD_DIM), F32),
            ((2 * n_glob, HEAD_DIM), BF),
        ],
        after=(picked,),
    )
    qo_glob = from_first(qo_pick)
    n_steps = total // QROWS
    base = (q, k, vt, bias, key_bias)
    stat_rows = ((n_steps, QROWS), F32)
    forward_types = [
        ((n_steps * N_KEYS, QROWS), BF),
        ((n_steps * HEAD_DIM, QROWS), F32),
        stat_rows,
        stat_rows,
    ]

    def window(name, body, args, state, outs, scratch=(), after=()):
        at = 1 + len(args)
        return local_call(
            name,
            body,
            ids,
            tuple(args) + tuple(state),
            outs,
            scratch,
            after=after,
            aliases={at + i: i for i in range(len(state))},
            mib=20,
        )

    seen = window(
        "forward_inner",
        functools.partial(window_forward_body, range(2, n_steps), False),
        base,
        (),
        forward_types,
    )
    win_weights, *seen = window(
        "forward_rim",
        functools.partial(window_forward_body, range(0, 2), True),
        base + (rim,),
        seen,
        forward_types,
    )
    attn, glob_weights, d_win, d_glob, delta_win, delta_glob = local_call(
        "glob_forward",
        glob_forward_body,
        ids,
        (q, d_attn, kv_glob, *seen),
        [
            head_rows,
            ((n_steps * n_glob, QROWS), BF),
            head_rows,
            head_rows,
            stat_rows,
            stat_rows,
        ],
        mib=20,
    )
    backward = (q, d_win, kt, v, win_weights, delta_win)
    dq_rim, *state, rim_sum = window(
        "backward_rim",
        functools.partial(window_backward_body, range(0, 2), True),
        backward + (rim,),
        (),
        [((2 * HEAD_DIM, QROWS), F32), head_sums, head_sums, ((2 * RIM, HEAD_DIM), BF)],
        [pltpu.VMEM((RIM, HEAD_DIM), F32)] * 2,
    )
    rim_back = to_next_group(rim_sum, -1)
    packed_rows = ((HEAD_DIM + 16, n_glob), BF)
    mine = local_call(
        "row_forward",
        row_forward_body,
        ids,
        (*qo_glob, k, v, vt),
        [packed_rows],
        [pltpu.VMEM((total, n_glob), F32)],
        after=(rim_sum,),
    )[0]
    d = 1
    while 2 * d < n_groups:
        mine = local_call("merge", merge_body, ids, (mine, with_group(mine, d)), [packed_rows])[0]
        d *= 2
    other = with_group(mine, d)
    dq_part, dkg, dvg = local_call(
        "glob_backward",
        glob_backward_body,
        ids,
        (q, d_glob, kv_glob, glob_weights, delta_glob),
        [((n_steps * HEAD_DIM, QROWS), F32), glob_sums, glob_sums],
        after=(mine,),
    )
    rk, rv, sums = local_call(
        "row_backward",
        row_backward_body,
        ids,
        (*qo_glob, k, v, kt, mine, other, dkg, dvg),
        [head_sums, head_sums, ((3 * n_glob, HEAD_DIM), BF)],
    )
    attn_parts = swap_in_group(
        local_call(
            "pack_rows",
            pack_rows_body,
            ids,
            (pos_row, attn, mine, other),
            [((tok, HEAD_DIM), BF)] * heads,
            [pltpu.VMEM((total, HEAD_DIM), BF)],
            after=(sums,),
        )
    )
    dk, dv, dq = window(
        "backward_inner",
        functools.partial(window_backward_body, range(2, n_steps), False),
        backward + (dq_part, dq_rim),
        state,
        [head_sums, head_sums, head_rows],
        after=(attn_parts[0],),
    )

    def to_lower(x, d):
        route = [
            (g * heads + j, (g - d) * heads + j)
            for g in range(d, min(2 * d, n_groups))
            for j in range(heads)
        ]
        return lax.ppermute(x, "seq", route)

    d = n_groups // 2
    while d > 1:
        sums = (sums.astype(F32) + to_lower(sums, d).astype(F32)).astype(BF)
        d //= 2
    other_sums = to_lower(sums, 1)
    grads = swap_in_group(
        local_call(
            "pack_grads",
            pack_grads_body,
            ids,
            (pos_row, dq, dk, dv, rk, rv, rim_back, sums, other_sums),
            [((3 * tok, HEAD_DIM), BF)] * heads,
            [
                pltpu.VMEM((total, HEAD_DIM), BF),
                pltpu.VMEM((total, HEAD_DIM), F32),
                pltpu.VMEM((total, HEAD_DIM), F32),
            ],
        )
    )
    n_head = lax.axis_size("head")
    out_cols = out_weight.shape[1] // n_head
    keep, send = local_call(
        "project",
        project_body,
        ids,
        (out_weight, *attn_parts),
        [((2, tok, out_cols), BF)] * 2,
        [pltpu.VMEM((tok, cols), BF)],
        after=(grads[0],),
    )
    half = lax.ppermute(send, "head", [(h, h ^ 1) for h in range(n_head)])
    summed = keep.astype(F32) + half.astype(F32)
    far = lax.ppermute(summed[1].astype(BF), "head", [(h, h ^ 2) for h in range(n_head)])
    layer_out = (summed[0] + far.astype(F32)).astype(BF)
    grad_queries, grad_keys, grad_values = local_call(
        "join_grads", join_grads_body, ids, tuple(grads), [((tok, cols), BF)] * 3, us=JOIN_US
    )
    return (layer_out, grad_queries, grad_keys, grad_values)


def solution(mesh):
    return jax.shard_map(
        on_device,
        mesh=mesh,
        in_specs=(
            P("seq", "head"),
            P("seq", "head"),
            P("seq", "head"),
            P("head", None),
            P("seq", None),
            P(),
            P("seq", None),
        ),
        out_specs=(P("seq", "head"), P("seq", "head"), P("seq", "head"), P("seq", "head")),
        check_vma=False,
    )
```

```python
import functools
import math

import jax
import jax.numpy as jnp
from jax import lax
from jax.experimental import pallas as pl
from jax.experimental.pallas import tpu as pltpu
from jax.sharding import PartitionSpec as P

HEAD_DIM = 128
BLOCK = 128
WBLK = 4
RIM = (WBLK - 1) * BLOCK
QROWS = 2 * BLOCK
SCALE = 1.0 / math.sqrt(HEAD_DIM)
SCALE2 = SCALE * math.log2(math.e)
BF = jnp.bfloat16
F32 = jnp.float32
NEG = float("-inf")
FLOOR = -1e30
JOIN_US = 12.0
PACK_MIB = 14


def nn(a, b):
    return lax.dot_general(a, b, (((1,), (0,)), ((), ())), preferred_element_type=F32)


def nt(a, b):
    return lax.dot_general(a, b, (((1,), (1,)), ((), ())), preferred_element_type=F32)


def rows(slot, count):
    return pl.ds(pl.multiple_of(slot * count, count), count)


def local_call(name, body, ids, arrays, outs, scratch=(), after=(), aliases=None, far=(), mib=14, us=0.0, out_space=pltpu.VMEM):
    first = 1 + len(arrays) + len(far)

    def kernel(*refs):
        body(*refs[:first], *refs[first + len(after) :])

    return pl.pallas_call(
        kernel,
        name=name,
        out_shape=tuple(jax.ShapeDtypeStruct(s, t) for s, t in outs),
        in_specs=[pl.BlockSpec(memory_space=pltpu.SMEM)]
        + [pl.BlockSpec(memory_space=pltpu.VMEM)] * len(arrays)
        + [pl.BlockSpec(memory_space=space) for _, space in far]
        + [pl.BlockSpec(memory_space=pl.ANY)] * len(after),
        out_specs=tuple(pl.BlockSpec(memory_space=out_space) for _ in outs),
        scratch_shapes=list(scratch),
        compiler_params=pltpu.CompilerParams(vmem_limit_bytes=mib * 2**20),
        input_output_aliases=aliases or {},
        cost_estimate=pl.CostEstimate(
            flops=1000 + int(us * 1.15e9), bytes_accessed=1000, transcendentals=0
        ),
    )(ids, *arrays, *[array for array, _ in far], *after)


def in_hbm(x):
    return pltpu.with_memory_space_constraint(x, pltpu.HBM)


def pack_kv_body(ids, k, v, *refs):
    outs, sems = refs[:-1], refs[-1]
    tok = k.shape[0]
    copies = []
    for i, out in enumerate(outs):
        col = rows(ids[0] ^ i, HEAD_DIM)
        copies += [
            pltpu.make_async_copy(k.at[:, col], out.at[0:tok, :], sems.at[2 * i]),
            pltpu.make_async_copy(v.at[:, col], out.at[tok:, :], sems.at[2 * i + 1]),
        ]
    for copy in copies:
        copy.start()
    for copy in copies:
        copy.wait()


def pack_qo_body(ids, q, out_grad, out_weight, block_mask, *refs):
    outs, d_attn = refs[:-1], refs[-1]
    tok = q.shape[0]
    entries = outs[0].shape[0] - 2 * tok
    at = lax.broadcasted_iota(jnp.int32, (entries, HEAD_DIM), 0)
    mask = jnp.zeros((entries, HEAD_DIM), jnp.int32)
    for e in range(entries):
        mask = jnp.where(at == e, block_mask[e // WBLK, e % WBLK], mask)
    mask = mask.astype(F32).astype(BF)
    d_attn[...] = nt(out_grad[...], out_weight[...]).astype(BF)
    for i, out in enumerate(outs):
        col = rows(ids[0] ^ i, HEAD_DIM)
        out[0:tok, :] = q[:, col]
        out[tok : 2 * tok, :] = d_attn[:, col]
        out[2 * tok :, :] = mask


def pick_rows(pos_col, tok):
    hits = pos_col == lax.broadcasted_iota(jnp.int32, (pos_col.shape[0], tok), 1)
    return hits.astype(BF)


def place_rows(pos_row, tok):
    return lax.broadcasted_iota(jnp.int32, (tok, pos_row.shape[1]), 0) == pos_row


def row_column(pos_row, tok):
    hit = place_rows(pos_row, tok).astype(F32)
    return jnp.max(hit, axis=1, keepdims=True) > 0.5


def join_kv_body(ids, pos_col, pos_row, *refs):
    pieces, (k, v, key_bias, picked, rim) = refs[:-5], refs[-5:]
    tok = k.shape[0] // len(pieces)
    for i, piece in enumerate(pieces):
        slot = ids[0] ^ i
        k[rows(slot, tok), :] = piece[0:tok, :]
        v[rows(slot, tok), :] = piece[tok:, :]
    picks = pick_rows(pos_col[...], tok)
    n = pos_col.shape[0]
    picked[0:n, :] = nn(picks, k[0:tok, :]).astype(BF)
    picked[n:, :] = nn(picks, v[0:tok, :]).astype(BF)
    rim[0:RIM, :] = k[k.shape[0] - RIM :, :]
    rim[RIM:, :] = v[k.shape[0] - RIM :, :]
    hidden = jnp.logical_and(row_column(pos_row[...], tok), ids[1] == 0)
    key_bias[...] = jnp.where(hidden, NEG, jnp.zeros(key_bias.shape, F32))


def turn_body(ids, k, v, kt, vt):
    kt[...] = k[...].T
    vt[...] = v[...].T


def join_qo_body(ids, pos_col, pos_row, *refs):
    pieces, (q, d_attn, bias, picked) = refs[:-4], refs[-4:]
    tok = q.shape[0] // len(pieces)
    n_rows = bias.shape[0] // len(pieces)
    n = pos_col.shape[0]
    for i, piece in enumerate(pieces):
        slot = ids[0] ^ i
        q[rows(slot, tok), :] = piece[0:tok, :]
        d_attn[rows(slot, tok), :] = piece[tok : 2 * tok, :]
        open_ = piece[2 * tok :, :].astype(F32)
        entry = lax.broadcasted_iota(jnp.int32, open_.shape, 0) + slot * n_rows
        inside = (ids[1] > 0) | (entry // WBLK >= entry % WBLK)
        bias[rows(slot, n_rows), :] = jnp.where((open_ > 0.5) & inside, 0.0, NEG)

    @pl.when(ids[1] == 0)
    def _():
        picks = pick_rows(pos_col[...], tok)
        picked[0:n, :] = nn(picks, q[0:tok, :]).astype(BF)
        picked[n:, :] = nn(picks, d_attn[0:tok, :]).astype(BF)
        is_row = row_column(pos_row[...], tok)
        kept = jnp.where(is_row, 0.0, d_attn[0:tok, :].astype(F32))
        d_attn[0:tok, :] = kept.astype(BF)

    @pl.when(ids[1] > 0)
    def _():
        picked[...] = jnp.zeros_like(picked)


def row_forward_body(ids, own, sent, k, v, vt, mine, scores):
    picked = ours(ids, own, sent)
    n = picked.shape[0] // 2
    step = 512
    query, d_out = picked[0:n, :], picked[n:, :]
    peak = None
    for c in range(0, k.shape[0], step):
        s = nt(k[c : c + step, :], query) * SCALE2
        scores[c : c + step, :] = s
        top = jnp.max(s, axis=0, keepdims=True)
        peak = top if peak is None else jnp.maximum(peak, top)
    mass = jnp.zeros((1, n), F32)
    dot = jnp.zeros((1, n), F32)
    numer = jnp.zeros((HEAD_DIM, n), F32)
    for c in range(0, k.shape[0], step):
        e = jnp.exp2(scores[c : c + step, :] - peak)
        vals = v[c : c + step, :]
        mass = mass + jnp.sum(e, axis=0, keepdims=True)
        dot = dot + jnp.sum(e * nt(vals, d_out), axis=0, keepdims=True)
        numer = numer + nn(vt[:, c : c + step], e.astype(BF))
    mine[0:HEAD_DIM, :] = (numer / mass).astype(BF)
    mine[HEAD_DIM:, :] = in_thirds((peak, mass, dot))


def in_thirds(values):
    parts = []
    for value in values:
        for _ in range(3):
            part = value.astype(BF).astype(F32)
            parts.append(part)
            value = value - part
    empty = jnp.zeros((16 - len(parts), parts[0].shape[1]), F32)
    return jnp.concatenate(parts + [empty], axis=0).astype(BF)


def merged(mine, other):
    thirds = [ref[HEAD_DIM:, :].astype(F32) for ref in (mine, other)]
    (pa, ma, da), (pb, mb, db) = [
        [t[3 * i : 3 * i + 1] + t[3 * i + 1 : 3 * i + 2] + t[3 * i + 2 : 3 * i + 3] for i in range(3)]
        for t in thirds
    ]
    peak = jnp.maximum(pa, pb)
    wa, wb = jnp.exp2(pa - peak), jnp.exp2(pb - peak)
    mass = ma * wa + mb * wb
    return peak, mass, da * wa + db * wb, ma * wa / mass, mb * wb / mass


def merged_attn(mine, other, wa, wb):
    both = mine[0:HEAD_DIM, :].astype(F32) * wa + other[0:HEAD_DIM, :].astype(F32) * wb
    return both.astype(BF)


def merge_body(ids, mine, other, out):
    peak, mass, dot, wa, wb = merged(mine, other)
    out[0:HEAD_DIM, :] = merged_attn(mine, other, wa, wb)
    out[HEAD_DIM:, :] = in_thirds((peak, mass, dot))


N_KEYS = RIM + QROWS


def window_span(sb):
    first = sb * QROWS - RIM
    cut = max(0, -first)
    return first, cut, slice(first + cut, (sb + 1) * QROWS)


def window_rows(sb, own, rim):
    _, cut, inner = window_span(sb)
    if not cut:
        return own[inner, :]
    return jnp.concatenate([rim[RIM - cut : RIM, :], own[inner, :]], axis=0)


def window_cols(sb, own_t, rim):
    _, cut, inner = window_span(sb)
    if not cut:
        return own_t[:, inner]
    return jnp.concatenate([rim[RIM - cut : RIM, :].T, own_t[:, inner]], axis=1)


def window_forward_body(steps, with_rim, ids, *refs):
    q, k, vt, bias, key_bias = refs[:5]
    k_rim, v_rim = (refs[5].at[0:RIM], refs[5].at[RIM:]) if with_rim else (None, None)
    weights, out_t, peaks, masses = refs[-4:]
    key_in = lax.broadcasted_iota(jnp.int32, (BLOCK, QROWS), 0)
    query_in = lax.broadcasted_iota(jnp.int32, (BLOCK, QROWS), 1)
    shut = jnp.full((1, BLOCK), NEG, F32)
    for sb in steps:
        here = slice(sb * QROWS, (sb + 1) * QROWS)
        first = window_span(sb)[0]
        kw, vwt = window_rows(sb, k, k_rim), window_cols(sb, vt, v_rim)
        raw = nt(kw, q[here, :])
        parts = []
        for kb in range(N_KEYS // BLOCK):
            halves = []
            for half in range(QROWS // BLOCK):
                r = half + WBLK - 1 - kb
                at = (sb * (QROWS // BLOCK) + half) * WBLK + r
                halves.append(bias[at : at + 1, :] if 0 <= r < WBLK else shut)
            part = raw[kb * BLOCK : (kb + 1) * BLOCK, :] * SCALE2 + jnp.concatenate(halves, axis=1)
            at = first + kb * BLOCK
            if 0 <= at < key_bias.shape[0]:
                col = key_bias[at : at + BLOCK, :]
                part = part + jnp.concatenate([col] * (QROWS // BLOCK), axis=1)
            own = kb - (WBLK - 1)
            if own >= 0:
                part = jnp.where(query_in - key_in >= own * BLOCK, part, NEG)
            parts.append(part)
        peak = jnp.full((1, QROWS), FLOOR, F32)
        for part in parts:
            peak = jnp.maximum(peak, part.max(axis=0, keepdims=True))
        grown = [jnp.exp2(part - peak) for part in parts]
        masses[sb : sb + 1, :] = sum(e.sum(axis=0, keepdims=True) for e in grown)
        peaks[sb : sb + 1, :] = peak
        ww = jnp.concatenate([e.astype(BF) for e in grown], axis=0)
        weights[sb * N_KEYS : (sb + 1) * N_KEYS, :] = ww
        out_t[sb * HEAD_DIM : (sb + 1) * HEAD_DIM, :] = nn(vwt, ww)


def ours(ids, mine, sent):
    return jnp.where(ids[1] < ids[3], mine[...], sent[...])


def glob_forward_body(ids, q, d_out, picked, out_t, peaks, masses, *refs):
    attn, weights, d_win, d_glob, delta_win, delta_glob = refs
    n = picked.shape[0] // 2
    kg, vgt = picked[0:n, :], picked[n:, :].T
    for sb in range(peaks.shape[0]):
        here = slice(sb * QROWS, (sb + 1) * QROWS)
        row = slice(sb, sb + 1)
        score = nt(kg, q[here, :]) * SCALE2
        peak = jnp.maximum(peaks[row, :], score.max(axis=0, keepdims=True))
        grown = jnp.exp2(score - peak)
        part = jnp.exp2(peaks[row, :] - peak)
        inv = 1.0 / (masses[row, :] * part + grown.sum(axis=0, keepdims=True))
        part = part * inv
        wg = grown.astype(BF)
        weights[sb * n : (sb + 1) * n, :] = wg
        both = out_t[sb * HEAD_DIM : (sb + 1) * HEAD_DIM, :] * part + nn(vgt, wg) * inv
        attn[here, :] = both.T.astype(BF)
        d_t = d_out[here, :].astype(F32).T
        delta = jnp.sum(both.astype(BF).astype(F32) * d_t, axis=0, keepdims=True)
        d_win[here, :] = (d_t * part).T.astype(BF)
        d_glob[here, :] = (d_t * inv).T.astype(BF)
        delta_win[row, :] = delta * part
        delta_glob[row, :] = delta * inv


def glob_backward_body(ids, q, d_out, picked, weights, delta, dq_part, dk_glob, dv_glob):
    n = picked.shape[0] // 2
    n_steps = delta.shape[0]
    kt, vg = picked[0:n, :].T, picked[n:, :]
    wide = 2
    dkg = jnp.zeros(dk_glob.shape, F32)
    dvg = jnp.zeros(dv_glob.shape, F32)
    for c in range(0, n_steps, wide):
        here = slice(c * QROWS, (c + wide) * QROWS)
        qb, dob = q[here, :], d_out[here, :]
        wg = jnp.concatenate(
            [weights[sb * n : (sb + 1) * n, :] for sb in range(c, c + wide)], axis=1
        )
        off = jnp.concatenate([delta[sb : sb + 1, :] for sb in range(c, c + wide)], axis=1)
        dg = (wg.astype(F32) * (nt(vg, dob) - off)).astype(BF)
        dq_t = nn(kt, dg)
        for i in range(wide):
            dq_part[(c + i) * HEAD_DIM : (c + i + 1) * HEAD_DIM, :] = dq_t[:, i * QROWS : (i + 1) * QROWS]
        dkg = dkg + nn(dg, qb)
        dvg = dvg + nn(wg, dob)
    dk_glob[...] = dkg
    dv_glob[...] = dvg


def window_backward_body(steps, with_rim, ids, *refs):
    q, d_out, kt, v, weights, delta = refs[:6]
    k_rim, v_rim = (refs[6].at[0:RIM], refs[6].at[RIM:]) if with_rim else (None, None)
    if with_rim:
        dq_rim, dk, dv, rim_back, dk_rim, dv_rim = refs[-6:]
        for ref in (dk, dv, dk_rim, dv_rim):
            ref[...] = jnp.zeros_like(ref)
    else:
        dq_part, dq_rim = refs[6:8]
        dk, dv, dq = refs[-3:]
        for sb in range(dq_rim.shape[0] // HEAD_DIM):
            here = slice(sb * HEAD_DIM, (sb + 1) * HEAD_DIM)
            dq_t = dq_rim[here, :] + dq_part[here, :]
            dq[sb * QROWS : (sb + 1) * QROWS, :] = (dq_t.T * SCALE).astype(BF)
    for sb in steps:
        here = slice(sb * QROWS, (sb + 1) * QROWS)
        _, cut, inner = window_span(sb)
        kwt, vw = window_cols(sb, kt, k_rim), window_rows(sb, v, v_rim)
        qb, dob = q[here, :], d_out[here, :]
        ww = weights[sb * N_KEYS : (sb + 1) * N_KEYS, :]
        dw = (ww.astype(F32) * (nt(vw, dob) - delta[sb : sb + 1, :])).astype(BF)
        part = slice(sb * HEAD_DIM, (sb + 1) * HEAD_DIM)
        if with_rim:
            dq_rim[part, :] = nn(kwt, dw)
        else:
            dq_t = nn(kwt, dw) + dq_part[part, :]
            dq[here, :] = (dq_t.T * SCALE).astype(BF)
        dkw, dvw = nn(dw, qb), nn(ww, dob)
        if cut:
            dk_rim[RIM - cut :, :] += dkw[0:cut, :]
            dv_rim[RIM - cut :, :] += dvw[0:cut, :]
        dk[inner, :] += dkw[cut:, :]
        dv[inner, :] += dvw[cut:, :]
    if with_rim:
        rim_back[0:RIM, :] = dk_rim[...].astype(BF)
        rim_back[RIM:, :] = dv_rim[...].astype(BF)


def row_backward_body(ids, own, sent, k, v, kt, mine, other, dkg, dvg, dk, dv, sums):
    picked = ours(ids, own, sent)
    n = picked.shape[0] // 2
    step = 512
    query, d_out = picked[0:n, :], picked[n:, :]
    peak, mass, dot, _, _ = merged(mine, other)
    lse = peak + jnp.log2(mass)
    delta = dot / mass
    dq_t = jnp.zeros((HEAD_DIM, n), F32)
    for c in range(0, k.shape[0], step):
        keys, vals = k[c : c + step, :], v[c : c + step, :]
        prob = jnp.exp2(nt(keys, query) * SCALE2 - lse)
        ds = (prob * (nt(vals, d_out) - delta)).astype(BF)
        dk[c : c + step, :] = nn(ds, query)
        dv[c : c + step, :] = nn(prob.astype(BF), d_out)
        dq_t = dq_t + nn(kt[:, c : c + step], ds)
    sums[0:n, :] = (dq_t.T * SCALE).astype(BF)
    sums[n : 2 * n, :] = dkg[...].astype(BF)
    sums[2 * n :, :] = dvg[...].astype(BF)


def pack_rows_body(ids, pos_row, attn, mine, other, *refs):
    outs, attn_f = refs[:-1], refs[-1]
    tok = attn.shape[0] // len(outs)
    attn_f[...] = attn[...]

    @pl.when(ids[1] == 0)
    def _():
        _, _, _, wa, wb = merged(mine, other)
        both_t = merged_attn(mine, other, wa, wb)
        hit = place_rows(pos_row[...], tok)
        is_row = jnp.max(hit.astype(F32), axis=1, keepdims=True) > 0.5
        placed = nt(hit.astype(BF), both_t)
        attn_f[0:tok, :] = jnp.where(is_row, placed, attn[0:tok, :].astype(F32)).astype(BF)

    for i, out in enumerate(outs):
        out[...] = attn_f[rows(ids[0] ^ i, tok), :]


def project_body(ids, w, *refs):
    pieces, (keep, send, attn) = refs[:-3], refs[-3:]
    for i, piece in enumerate(pieces):
        attn[:, rows(ids[0] ^ i, HEAD_DIM)] = piece[...]
    cols = keep.shape[2]
    a = attn[...]
    me = ids[2]
    for i, group in enumerate((me, me ^ 2)):
        keep[i] = nn(a, w[:, rows(group, cols)]).astype(BF)
    for i, group in enumerate((me ^ 1, me ^ 3)):
        send[i] = nn(a, w[:, rows(group, cols)]).astype(BF)


def pack_grads_body(ids, pos_row, dq, dk, dv, rk, rv, rim_back, sums, other, *refs):
    outs, (dqf, dkf, dvf) = refs[:-3], refs[-3:]
    total = dk.shape[0]
    tok = total // len(outs)
    n = sums.shape[0] // 3
    dqf[...] = dq[...]
    dkf[...] = dk[...] + rk[...]
    dvf[...] = dv[...] + rv[...]
    dkf[total - RIM :, :] += rim_back[0:RIM, :].astype(F32)
    dvf[total - RIM :, :] += rim_back[RIM:, :].astype(F32)

    @pl.when(ids[1] == 0)
    def _():
        both = (sums[...].astype(F32) + other[...].astype(F32)).astype(BF)
        hit = place_rows(pos_row[...], tok).astype(BF)
        dqf[0:tok, :] = (dqf[0:tok, :].astype(F32) + nn(hit, both[0:n, :])).astype(BF)
        dkf[0:tok, :] += nn(hit, both[n : 2 * n, :])
        dvf[0:tok, :] += nn(hit, both[2 * n :, :])

    for i, out in enumerate(outs):
        here = rows(ids[0] ^ i, tok)
        out[0:tok, :] = dqf[here, :]
        out[tok : 2 * tok, :] = (dkf[here, :] * SCALE).astype(BF)
        out[2 * tok :, :] = dvf[here, :].astype(BF)


def join_grads_body(ids, *refs):
    pieces, outs = refs[:-3], refs[-3:]
    tok = outs[0].shape[0]
    for i, piece in enumerate(pieces):
        col = rows(ids[0] ^ i, HEAD_DIM)
        for at, out in enumerate(outs):
            out[:, col] = piece[at * tok : (at + 1) * tok, :]


def on_device(queries, keys, values, out_weight, out_grad, global_pos, block_mask):
    tok, cols = queries.shape
    heads = cols // HEAD_DIM
    n_seq = lax.axis_size("seq")
    n_groups = n_seq // heads
    total = heads * tok
    n_glob = global_pos.shape[0]
    seq_index = lax.axis_index("seq")
    group = seq_index // heads
    last = 1
    while 2 * last < n_groups:
        last *= 2
    ids = jnp.stack([seq_index % heads, group, lax.axis_index("head"), jnp.int32(last)])
    ids = ids.astype(jnp.int32)
    pos_col = global_pos.reshape(n_glob, 1)
    pos_row = global_pos.reshape(1, n_glob)

    def swap_in_group(pieces):
        moved = [
            lax.ppermute(piece, "seq", [(s, s ^ i) for s in range(n_seq)])
            for i, piece in enumerate(pieces)
            if i
        ]
        return [pieces[0]] + moved

    def from_first(x):
        d = 1
        while True:
            route = [
                (g * heads + j, (g + d) * heads + j)
                for g in range(d)
                for j in range(heads)
                if g + d < n_groups
            ]
            sent = lax.ppermute(x, "seq", route)
            if 2 * d >= n_groups:
                return x, sent
            x = jnp.where((group >= d) & (group < 2 * d), sent, x)
            d *= 2

    def to_next_group(x, step):
        route = [(s, s + step * heads) for s in range(n_seq) if 0 <= s + step * heads < n_seq]
        return lax.ppermute(x, "seq", route)

    def with_group(x, d):
        return lax.ppermute(x, "seq", [(s, s ^ (d * heads)) for s in range(n_seq)])

    kv_packed = local_call(
        "pack_kv",
        pack_kv_body,
        ids,
        (),
        [((2 * tok, HEAD_DIM), BF)] * heads,
        [pltpu.SemaphoreType.DMA((2 * heads,))],
        far=((in_hbm(keys), pltpu.HBM), (in_hbm(values), pltpu.HBM)),
        mib=PACK_MIB,
        out_space=pltpu.VMEM,
    )
    kv = swap_in_group(kv_packed)
    qo = swap_in_group(
        local_call(
            "pack_qo",
            pack_qo_body,
            ids,
            (queries, out_grad, out_weight),
            [((2 * tok + block_mask.size, HEAD_DIM), BF)] * heads,
            [pltpu.VMEM((tok, cols), BF)],
            far=((block_mask, pltpu.SMEM),),
            after=(kv_packed[0],),
        )
    )
    head_rows = ((total, HEAD_DIM), BF)
    head_sums = ((total, HEAD_DIM), F32)
    glob_sums = ((n_glob, HEAD_DIM), F32)
    k, v, key_bias, picked, rim_out = local_call(
        "join_kv",
        join_kv_body,
        ids,
        (pos_col, pos_row, *kv),
        [
            head_rows,
            head_rows,
            ((tok, HEAD_DIM), F32),
            ((2 * n_glob, HEAD_DIM), BF),
            ((2 * RIM, HEAD_DIM), BF),
        ],
    )
    kv_own, kv_sent = from_first(picked)
    kv_glob = jnp.where(group >= last, kv_sent, kv_own)
    kt, vt = local_call("turn", turn_body, ids, (k, v), [((HEAD_DIM, total), BF)] * 2)
    rim_out, qo[2] = lax.optimization_barrier((rim_out, qo[2]))
    rim = to_next_group(rim_out, 1)
    q, d_attn, bias, qo_pick = local_call(
        "join_qo",
        join_qo_body,
        ids,
        (pos_col, pos_row, *qo),
        [
            head_rows,
            head_rows,
            ((heads * block_mask.size, HEAD_DIM), F32),
            ((2 * n_glob, HEAD_DIM), BF),
        ],
        after=(picked,),
    )
    qo_glob = from_first(qo_pick)
    n_steps = total // QROWS
    base = (q, k, vt, bias, key_bias)
    stat_rows = ((n_steps, QROWS), F32)
    forward_types = [
        ((n_steps * N_KEYS, QROWS), BF),
        ((n_steps * HEAD_DIM, QROWS), F32),
        stat_rows,
        stat_rows,
    ]

    def window(name, body, args, state, outs, scratch=(), after=()):
        at = 1 + len(args)
        return local_call(
            name,
            body,
            ids,
            tuple(args) + tuple(state),
            outs,
            scratch,
            after=after,
            aliases={at + i: i for i in range(len(state))},
            mib=20,
        )

    seen = window(
        "forward_inner",
        functools.partial(window_forward_body, range(2, n_steps), False),
        base,
        (),
        forward_types,
    )
    win_weights, *seen = window(
        "forward_rim",
        functools.partial(window_forward_body, range(0, 2), True),
        base + (rim,),
        seen,
        forward_types,
    )
    attn, glob_weights, d_win, d_glob, delta_win, delta_glob = local_call(
        "glob_forward",
        glob_forward_body,
        ids,
        (q, d_attn, kv_glob, *seen),
        [
            head_rows,
            ((n_steps * n_glob, QROWS), BF),
            head_rows,
            head_rows,
            stat_rows,
            stat_rows,
        ],
        mib=20,
    )
    backward = (q, d_win, kt, v, win_weights, delta_win)
    dq_rim, *state, rim_sum = window(
        "backward_rim",
        functools.partial(window_backward_body, range(0, 2), True),
        backward + (rim,),
        (),
        [((2 * HEAD_DIM, QROWS), F32), head_sums, head_sums, ((2 * RIM, HEAD_DIM), BF)],
        [pltpu.VMEM((RIM, HEAD_DIM), F32)] * 2,
    )
    rim_back = to_next_group(rim_sum, -1)
    packed_rows = ((HEAD_DIM + 16, n_glob), BF)
    mine = local_call(
        "row_forward",
        row_forward_body,
        ids,
        (*qo_glob, k, v, vt),
        [packed_rows],
        [pltpu.VMEM((total, n_glob), F32)],
        after=(rim_sum,),
    )[0]
    d = 1
    while 2 * d < n_groups:
        mine = local_call("merge", merge_body, ids, (mine, with_group(mine, d)), [packed_rows])[0]
        d *= 2
    other = with_group(mine, d)
    dq_part, dkg, dvg = local_call(
        "glob_backward",
        glob_backward_body,
        ids,
        (q, d_glob, kv_glob, glob_weights, delta_glob),
        [((n_steps * HEAD_DIM, QROWS), F32), glob_sums, glob_sums],
        after=(mine,),
    )
    rk, rv, sums = local_call(
        "row_backward",
        row_backward_body,
        ids,
        (*qo_glob, k, v, kt, mine, other, dkg, dvg),
        [head_sums, head_sums, ((3 * n_glob, HEAD_DIM), BF)],
    )
    attn_parts = swap_in_group(
        local_call(
            "pack_rows",
            pack_rows_body,
            ids,
            (pos_row, attn, mine, other),
            [((tok, HEAD_DIM), BF)] * heads,
            [pltpu.VMEM((total, HEAD_DIM), BF)],
            after=(sums,),
        )
    )
    dk, dv, dq = window(
        "backward_inner",
        functools.partial(window_backward_body, range(2, n_steps), False),
        backward + (dq_part, dq_rim),
        state,
        [head_sums, head_sums, head_rows],
        after=(attn_parts[0],),
    )

    def to_lower(x, d):
        route = [
            (g * heads + j, (g - d) * heads + j)
            for g in range(d, min(2 * d, n_groups))
            for j in range(heads)
        ]
        return lax.ppermute(x, "seq", route)

    d = n_groups // 2
    while d > 1:
        sums = (sums.astype(F32) + to_lower(sums, d).astype(F32)).astype(BF)
        d //= 2
    other_sums = to_lower(sums, 1)
    grads = swap_in_group(
        local_call(
            "pack_grads",
            pack_grads_body,
            ids,
            (pos_row, dq, dk, dv, rk, rv, rim_back, sums, other_sums),
            [((3 * tok, HEAD_DIM), BF)] * heads,
            [
                pltpu.VMEM((total, HEAD_DIM), BF),
                pltpu.VMEM((total, HEAD_DIM), F32),
                pltpu.VMEM((total, HEAD_DIM), F32),
            ],
        )
    )
    n_head = lax.axis_size("head")
    out_cols = out_weight.shape[1] // n_head
    keep, send = local_call(
        "project",
        project_body,
        ids,
        (out_weight, *attn_parts),
        [((2, tok, out_cols), BF)] * 2,
        [pltpu.VMEM((tok, cols), BF)],
        after=(grads[0],),
    )
    half = lax.ppermute(send, "head", [(h, h ^ 1) for h in range(n_head)])
    summed = keep.astype(F32) + half.astype(F32)
    far = lax.ppermute(summed[1].astype(BF), "head", [(h, h ^ 2) for h in range(n_head)])
    layer_out = (summed[0] + far.astype(F32)).astype(BF)
    grad_queries, grad_keys, grad_values = local_call(
        "join_grads", join_grads_body, ids, tuple(grads), [((tok, cols), BF)] * 3, us=JOIN_US
    )
    return (layer_out, grad_queries, grad_keys, grad_values)


def solution(mesh):
    return jax.shard_map(
        on_device,
        mesh=mesh,
        in_specs=(
            P("seq", "head"),
            P("seq", "head"),
            P("seq", "head"),
            P("head", None),
            P("seq", None),
            P(),
            P("seq", None),
        ),
        out_specs=(P("seq", "head"), P("seq", "head"), P("seq", "head"), P("seq", "head")),
        check_vma=False,
    )
```

```python
import functools
import math

import jax
import jax.numpy as jnp
from jax import lax
from jax.experimental import pallas as pl
from jax.experimental.pallas import tpu as pltpu
from jax.sharding import PartitionSpec as P

HEAD_DIM = 128
BLOCK = 128
WBLK = 4
RIM = (WBLK - 1) * BLOCK
QROWS = 2 * BLOCK
SCALE = 1.0 / math.sqrt(HEAD_DIM)
SCALE2 = SCALE * math.log2(math.e)
BF = jnp.bfloat16
F32 = jnp.float32
NEG = float("-inf")
FLOOR = -1e30
JOIN_US = 12.0
PACK_MIB = 14


def nn(a, b):
    return lax.dot_general(a, b, (((1,), (0,)), ((), ())), preferred_element_type=F32)


def nt(a, b):
    return lax.dot_general(a, b, (((1,), (1,)), ((), ())), preferred_element_type=F32)


def rows(slot, count):
    return pl.ds(pl.multiple_of(slot * count, count), count)


def local_call(name, body, ids, arrays, outs, scratch=(), after=(), aliases=None, far=(), mib=14, us=0.0, out_space=pltpu.VMEM):
    first = 1 + len(arrays) + len(far)

    def kernel(*refs):
        body(*refs[:first], *refs[first + len(after) :])

    return pl.pallas_call(
        kernel,
        name=name,
        out_shape=tuple(jax.ShapeDtypeStruct(s, t) for s, t in outs),
        in_specs=[pl.BlockSpec(memory_space=pltpu.SMEM)]
        + [pl.BlockSpec(memory_space=pltpu.VMEM)] * len(arrays)
        + [pl.BlockSpec(memory_space=space) for _, space in far]
        + [pl.BlockSpec(memory_space=pl.ANY)] * len(after),
        out_specs=tuple(pl.BlockSpec(memory_space=out_space) for _ in outs),
        scratch_shapes=list(scratch),
        compiler_params=pltpu.CompilerParams(vmem_limit_bytes=mib * 2**20),
        input_output_aliases=aliases or {},
        cost_estimate=pl.CostEstimate(
            flops=1000 + int(us * 1.15e9), bytes_accessed=1000, transcendentals=0
        ),
    )(ids, *arrays, *[array for array, _ in far], *after)


def in_hbm(x):
    return pltpu.with_memory_space_constraint(x, pltpu.HBM)


def pack_kv_body(ids, k, v, *refs):
    outs, sems = refs[:-1], refs[-1]
    tok = k.shape[0]
    copies = []
    for i, out in enumerate(outs):
        col = rows(ids[0] ^ i, HEAD_DIM)
        copies += [
            pltpu.make_async_copy(k.at[:, col], out.at[0:tok, :], sems.at[2 * i]),
            pltpu.make_async_copy(v.at[:, col], out.at[tok:, :], sems.at[2 * i + 1]),
        ]
    for copy in copies:
        copy.start()
    for copy in copies:
        copy.wait()


def pack_qo_body(ids, q, out_grad, out_weight, block_mask, *refs):
    outs, d_attn = refs[:-1], refs[-1]
    tok = q.shape[0]
    entries = outs[0].shape[0] - 2 * tok
    at = lax.broadcasted_iota(jnp.int32, (entries, HEAD_DIM), 0)
    mask = jnp.zeros((entries, HEAD_DIM), jnp.int32)
    for e in range(entries):
        mask = jnp.where(at == e, block_mask[e // WBLK, e % WBLK], mask)
    mask = mask.astype(F32).astype(BF)
    d_attn[...] = nt(out_grad[...], out_weight[...]).astype(BF)
    for i, out in enumerate(outs):
        col = rows(ids[0] ^ i, HEAD_DIM)
        out[0:tok, :] = q[:, col]
        out[tok : 2 * tok, :] = d_attn[:, col]
        out[2 * tok :, :] = mask


def pick_rows(pos_col, tok):
    hits = pos_col == lax.broadcasted_iota(jnp.int32, (pos_col.shape[0], tok), 1)
    return hits.astype(BF)


def place_rows(pos_row, tok):
    return lax.broadcasted_iota(jnp.int32, (tok, pos_row.shape[1]), 0) == pos_row


def row_column(pos_row, tok):
    hit = place_rows(pos_row, tok).astype(F32)
    return jnp.max(hit, axis=1, keepdims=True) > 0.5


def join_kv_body(ids, pos_col, pos_row, *refs):
    pieces, (k, v, key_bias, picked) = refs[:-4], refs[-4:]
    tok = k.shape[0] // len(pieces)
    for i, piece in enumerate(pieces):
        slot = ids[0] ^ i
        k[rows(slot, tok), :] = piece[0:tok, :]
        v[rows(slot, tok), :] = piece[tok:, :]
    picks = pick_rows(pos_col[...], tok)
    n = pos_col.shape[0]
    picked[0:n, :] = nn(picks, k[0:tok, :]).astype(BF)
    picked[n:, :] = nn(picks, v[0:tok, :]).astype(BF)
    hidden = jnp.logical_and(row_column(pos_row[...], tok), ids[1] == 0)
    key_bias[...] = jnp.where(hidden, NEG, jnp.zeros(key_bias.shape, F32))


def turn_body(ids, k, v, kt, vt, rim):
    kt[...] = k[...].T
    vt[...] = v[...].T
    rim[0:RIM, :] = k[k.shape[0] - RIM :, :]
    rim[RIM:, :] = v[k.shape[0] - RIM :, :]


def join_qo_body(ids, pos_col, pos_row, *refs):
    pieces, (q, d_attn, bias, picked) = refs[:-4], refs[-4:]
    tok = q.shape[0] // len(pieces)
    n_rows = bias.shape[0] // len(pieces)
    n = pos_col.shape[0]
    for i, piece in enumerate(pieces):
        slot = ids[0] ^ i
        q[rows(slot, tok), :] = piece[0:tok, :]
        d_attn[rows(slot, tok), :] = piece[tok : 2 * tok, :]
        open_ = piece[2 * tok :, :].astype(F32)
        entry = lax.broadcasted_iota(jnp.int32, open_.shape, 0) + slot * n_rows
        inside = (ids[1] > 0) | (entry // WBLK >= entry % WBLK)
        bias[rows(slot, n_rows), :] = jnp.where((open_ > 0.5) & inside, 0.0, NEG)

    @pl.when(ids[1] == 0)
    def _():
        picks = pick_rows(pos_col[...], tok)
        picked[0:n, :] = nn(picks, q[0:tok, :]).astype(BF)
        picked[n:, :] = nn(picks, d_attn[0:tok, :]).astype(BF)
        is_row = row_column(pos_row[...], tok)
        kept = jnp.where(is_row, 0.0, d_attn[0:tok, :].astype(F32))
        d_attn[0:tok, :] = kept.astype(BF)

    @pl.when(ids[1] > 0)
    def _():
        picked[...] = jnp.zeros_like(picked)


def row_forward_body(ids, own, sent, k, v, vt, mine, scores):
    picked = ours(ids, own, sent)
    n = picked.shape[0] // 2
    step = 512
    query, d_out = picked[0:n, :], picked[n:, :]
    peak = None
    for c in range(0, k.shape[0], step):
        s = nt(k[c : c + step, :], query) * SCALE2
        scores[c : c + step, :] = s
        top = jnp.max(s, axis=0, keepdims=True)
        peak = top if peak is None else jnp.maximum(peak, top)
    mass = jnp.zeros((1, n), F32)
    dot = jnp.zeros((1, n), F32)
    numer = jnp.zeros((HEAD_DIM, n), F32)
    for c in range(0, k.shape[0], step):
        e = jnp.exp2(scores[c : c + step, :] - peak)
        vals = v[c : c + step, :]
        mass = mass + jnp.sum(e, axis=0, keepdims=True)
        dot = dot + jnp.sum(e * nt(vals, d_out), axis=0, keepdims=True)
        numer = numer + nn(vt[:, c : c + step], e.astype(BF))
    mine[0:HEAD_DIM, :] = (numer / mass).astype(BF)
    mine[HEAD_DIM:, :] = in_thirds((peak, mass, dot))


def in_thirds(values):
    parts = []
    for value in values:
        for _ in range(3):
            part = value.astype(BF).astype(F32)
            parts.append(part)
            value = value - part
    empty = jnp.zeros((16 - len(parts), parts[0].shape[1]), F32)
    return jnp.concatenate(parts + [empty], axis=0).astype(BF)


def merged(mine, other):
    thirds = [ref[HEAD_DIM:, :].astype(F32) for ref in (mine, other)]
    (pa, ma, da), (pb, mb, db) = [
        [t[3 * i : 3 * i + 1] + t[3 * i + 1 : 3 * i + 2] + t[3 * i + 2 : 3 * i + 3] for i in range(3)]
        for t in thirds
    ]
    peak = jnp.maximum(pa, pb)
    wa, wb = jnp.exp2(pa - peak), jnp.exp2(pb - peak)
    mass = ma * wa + mb * wb
    return peak, mass, da * wa + db * wb, ma * wa / mass, mb * wb / mass


def merged_attn(mine, other, wa, wb):
    both = mine[0:HEAD_DIM, :].astype(F32) * wa + other[0:HEAD_DIM, :].astype(F32) * wb
    return both.astype(BF)


def merge_body(ids, mine, other, out):
    peak, mass, dot, wa, wb = merged(mine, other)
    out[0:HEAD_DIM, :] = merged_attn(mine, other, wa, wb)
    out[HEAD_DIM:, :] = in_thirds((peak, mass, dot))


N_KEYS = RIM + QROWS


def window_span(sb):
    first = sb * QROWS - RIM
    cut = max(0, -first)
    return first, cut, slice(first + cut, (sb + 1) * QROWS)


def window_rows(sb, own, rim):
    _, cut, inner = window_span(sb)
    if not cut:
        return own[inner, :]
    return jnp.concatenate([rim[RIM - cut : RIM, :], own[inner, :]], axis=0)


def window_cols(sb, own_t, rim):
    _, cut, inner = window_span(sb)
    if not cut:
        return own_t[:, inner]
    return jnp.concatenate([rim[RIM - cut : RIM, :].T, own_t[:, inner]], axis=1)


def window_forward_body(steps, with_rim, ids, *refs):
    q, k, vt, bias, key_bias = refs[:5]
    k_rim, v_rim = (refs[5].at[0:RIM], refs[5].at[RIM:]) if with_rim else (None, None)
    weights, out_t, peaks, masses = refs[-4:]
    key_in = lax.broadcasted_iota(jnp.int32, (BLOCK, QROWS), 0)
    query_in = lax.broadcasted_iota(jnp.int32, (BLOCK, QROWS), 1)
    shut = jnp.full((1, BLOCK), NEG, F32)
    for sb in steps:
        here = slice(sb * QROWS, (sb + 1) * QROWS)
        first = window_span(sb)[0]
        kw, vwt = window_rows(sb, k, k_rim), window_cols(sb, vt, v_rim)
        raw = nt(kw, q[here, :])
        parts = []
        for kb in range(N_KEYS // BLOCK):
            halves = []
            for half in range(QROWS // BLOCK):
                r = half + WBLK - 1 - kb
                at = (sb * (QROWS // BLOCK) + half) * WBLK + r
                halves.append(bias[at : at + 1, :] if 0 <= r < WBLK else shut)
            part = raw[kb * BLOCK : (kb + 1) * BLOCK, :] * SCALE2 + jnp.concatenate(halves, axis=1)
            at = first + kb * BLOCK
            if 0 <= at < key_bias.shape[0]:
                col = key_bias[at : at + BLOCK, :]
                part = part + jnp.concatenate([col] * (QROWS // BLOCK), axis=1)
            own = kb - (WBLK - 1)
            if own >= 0:
                part = jnp.where(query_in - key_in >= own * BLOCK, part, NEG)
            parts.append(part)
        peak = jnp.full((1, QROWS), FLOOR, F32)
        for part in parts:
            peak = jnp.maximum(peak, part.max(axis=0, keepdims=True))
        grown = [jnp.exp2(part - peak) for part in parts]
        masses[sb : sb + 1, :] = sum(e.sum(axis=0, keepdims=True) for e in grown)
        peaks[sb : sb + 1, :] = peak
        ww = jnp.concatenate([e.astype(BF) for e in grown], axis=0)
        weights[sb * N_KEYS : (sb + 1) * N_KEYS, :] = ww
        out_t[sb * HEAD_DIM : (sb + 1) * HEAD_DIM, :] = nn(vwt, ww)


def ours(ids, mine, sent):
    return jnp.where(ids[1] < ids[3], mine[...], sent[...])


def glob_forward_body(ids, q, d_out, picked, out_t, peaks, masses, *refs):
    attn, weights, d_win, d_glob, delta_win, delta_glob = refs
    n = picked.shape[0] // 2
    kg, vgt = picked[0:n, :], picked[n:, :].T
    for sb in range(peaks.shape[0]):
        here = slice(sb * QROWS, (sb + 1) * QROWS)
        row = slice(sb, sb + 1)
        score = nt(kg, q[here, :]) * SCALE2
        peak = jnp.maximum(peaks[row, :], score.max(axis=0, keepdims=True))
        grown = jnp.exp2(score - peak)
        part = jnp.exp2(peaks[row, :] - peak)
        inv = 1.0 / (masses[row, :] * part + grown.sum(axis=0, keepdims=True))
        part = part * inv
        wg = grown.astype(BF)
        weights[sb * n : (sb + 1) * n, :] = wg
        both = out_t[sb * HEAD_DIM : (sb + 1) * HEAD_DIM, :] * part + nn(vgt, wg) * inv
        attn[here, :] = both.T.astype(BF)
        d_t = d_out[here, :].astype(F32).T
        delta = jnp.sum(both.astype(BF).astype(F32) * d_t, axis=0, keepdims=True)
        d_win[here, :] = (d_t * part).T.astype(BF)
        d_glob[here, :] = (d_t * inv).T.astype(BF)
        delta_win[row, :] = delta * part
        delta_glob[row, :] = delta * inv


def glob_backward_body(ids, q, d_out, picked, weights, delta, dq_part, dk_glob, dv_glob):
    n = picked.shape[0] // 2
    n_steps = delta.shape[0]
    kt, vg = picked[0:n, :].T, picked[n:, :]
    wide = 2
    dkg = jnp.zeros(dk_glob.shape, F32)
    dvg = jnp.zeros(dv_glob.shape, F32)
    for c in range(0, n_steps, wide):
        here = slice(c * QROWS, (c + wide) * QROWS)
        qb, dob = q[here, :], d_out[here, :]
        wg = jnp.concatenate(
            [weights[sb * n : (sb + 1) * n, :] for sb in range(c, c + wide)], axis=1
        )
        off = jnp.concatenate([delta[sb : sb + 1, :] for sb in range(c, c + wide)], axis=1)
        dg = (wg.astype(F32) * (nt(vg, dob) - off)).astype(BF)
        dq_t = nn(kt, dg)
        for i in range(wide):
            dq_part[(c + i) * HEAD_DIM : (c + i + 1) * HEAD_DIM, :] = dq_t[:, i * QROWS : (i + 1) * QROWS]
        dkg = dkg + nn(dg, qb)
        dvg = dvg + nn(wg, dob)
    dk_glob[...] = dkg
    dv_glob[...] = dvg


def window_backward_body(steps, with_rim, ids, *refs):
    q, d_out, kt, v, weights, delta = refs[:6]
    k_rim, v_rim = (refs[6].at[0:RIM], refs[6].at[RIM:]) if with_rim else (None, None)
    if with_rim:
        dq_rim, dk, dv, rim_back, dk_rim, dv_rim = refs[-6:]
        for ref in (dk, dv, dk_rim, dv_rim):
            ref[...] = jnp.zeros_like(ref)
    else:
        dq_part, dq_rim = refs[6:8]
        dk, dv, dq = refs[-3:]
        for sb in range(dq_rim.shape[0] // HEAD_DIM):
            here = slice(sb * HEAD_DIM, (sb + 1) * HEAD_DIM)
            dq_t = dq_rim[here, :] + dq_part[here, :]
            dq[sb * QROWS : (sb + 1) * QROWS, :] = (dq_t.T * SCALE).astype(BF)
    for sb in steps:
        here = slice(sb * QROWS, (sb + 1) * QROWS)
        _, cut, inner = window_span(sb)
        kwt, vw = window_cols(sb, kt, k_rim), window_rows(sb, v, v_rim)
        qb, dob = q[here, :], d_out[here, :]
        ww = weights[sb * N_KEYS : (sb + 1) * N_KEYS, :]
        dw = (ww.astype(F32) * (nt(vw, dob) - delta[sb : sb + 1, :])).astype(BF)
        part = slice(sb * HEAD_DIM, (sb + 1) * HEAD_DIM)
        if with_rim:
            dq_rim[part, :] = nn(kwt, dw)
        else:
            dq_t = nn(kwt, dw) + dq_part[part, :]
            dq[here, :] = (dq_t.T * SCALE).astype(BF)
        dkw, dvw = nn(dw, qb), nn(ww, dob)
        if cut:
            dk_rim[RIM - cut :, :] += dkw[0:cut, :]
            dv_rim[RIM - cut :, :] += dvw[0:cut, :]
        dk[inner, :] += dkw[cut:, :]
        dv[inner, :] += dvw[cut:, :]
    if with_rim:
        rim_back[0:RIM, :] = dk_rim[...].astype(BF)
        rim_back[RIM:, :] = dv_rim[...].astype(BF)


def row_backward_body(ids, own, sent, k, v, kt, mine, other, dkg, dvg, dk, dv, sums):
    picked = ours(ids, own, sent)
    n = picked.shape[0] // 2
    step = 512
    query, d_out = picked[0:n, :], picked[n:, :]
    peak, mass, dot, _, _ = merged(mine, other)
    lse = peak + jnp.log2(mass)
    delta = dot / mass
    dq_t = jnp.zeros((HEAD_DIM, n), F32)
    for c in range(0, k.shape[0], step):
        keys, vals = k[c : c + step, :], v[c : c + step, :]
        prob = jnp.exp2(nt(keys, query) * SCALE2 - lse)
        ds = (prob * (nt(vals, d_out) - delta)).astype(BF)
        dk[c : c + step, :] = nn(ds, query)
        dv[c : c + step, :] = nn(prob.astype(BF), d_out)
        dq_t = dq_t + nn(kt[:, c : c + step], ds)
    sums[0:n, :] = (dq_t.T * SCALE).astype(BF)
    sums[n : 2 * n, :] = dkg[...].astype(BF)
    sums[2 * n :, :] = dvg[...].astype(BF)


def pack_rows_body(ids, pos_row, attn, mine, other, *refs):
    outs, attn_f = refs[:-1], refs[-1]
    tok = attn.shape[0] // len(outs)
    attn_f[...] = attn[...]

    @pl.when(ids[1] == 0)
    def _():
        _, _, _, wa, wb = merged(mine, other)
        both_t = merged_attn(mine, other, wa, wb)
        hit = place_rows(pos_row[...], tok)
        is_row = jnp.max(hit.astype(F32), axis=1, keepdims=True) > 0.5
        placed = nt(hit.astype(BF), both_t)
        attn_f[0:tok, :] = jnp.where(is_row, placed, attn[0:tok, :].astype(F32)).astype(BF)

    for i, out in enumerate(outs):
        out[...] = attn_f[rows(ids[0] ^ i, tok), :]


def project_body(ids, w, *refs):
    pieces, (keep, send, attn) = refs[:-3], refs[-3:]
    for i, piece in enumerate(pieces):
        attn[:, rows(ids[0] ^ i, HEAD_DIM)] = piece[...]
    cols = keep.shape[2]
    a = attn[...]
    me = ids[2]
    for i, group in enumerate((me, me ^ 2)):
        keep[i] = nn(a, w[:, rows(group, cols)]).astype(BF)
    for i, group in enumerate((me ^ 1, me ^ 3)):
        send[i] = nn(a, w[:, rows(group, cols)]).astype(BF)


def pack_grads_body(ids, pos_row, dq, dk, dv, rk, rv, rim_back, sums, other, *refs):
    outs, (dqf, dkf, dvf) = refs[:-3], refs[-3:]
    total = dk.shape[0]
    tok = total // len(outs)
    n = sums.shape[0] // 3
    dqf[...] = dq[...]
    dkf[...] = dk[...] + rk[...]
    dvf[...] = dv[...] + rv[...]
    dkf[total - RIM :, :] += rim_back[0:RIM, :].astype(F32)
    dvf[total - RIM :, :] += rim_back[RIM:, :].astype(F32)

    @pl.when(ids[1] == 0)
    def _():
        both = (sums[...].astype(F32) + other[...].astype(F32)).astype(BF)
        hit = place_rows(pos_row[...], tok).astype(BF)
        dqf[0:tok, :] = (dqf[0:tok, :].astype(F32) + nn(hit, both[0:n, :])).astype(BF)
        dkf[0:tok, :] += nn(hit, both[n : 2 * n, :])
        dvf[0:tok, :] += nn(hit, both[2 * n :, :])

    for i, out in enumerate(outs):
        here = rows(ids[0] ^ i, tok)
        out[0:tok, :] = dqf[here, :]
        out[tok : 2 * tok, :] = (dkf[here, :] * SCALE).astype(BF)
        out[2 * tok :, :] = dvf[here, :].astype(BF)


def join_grads_body(ids, *refs):
    pieces, outs = refs[:-3], refs[-3:]
    tok = outs[0].shape[0]
    for i, piece in enumerate(pieces):
        col = rows(ids[0] ^ i, HEAD_DIM)
        for at, out in enumerate(outs):
            out[:, col] = piece[at * tok : (at + 1) * tok, :]


def on_device(queries, keys, values, out_weight, out_grad, global_pos, block_mask):
    tok, cols = queries.shape
    heads = cols // HEAD_DIM
    n_seq = lax.axis_size("seq")
    n_groups = n_seq // heads
    total = heads * tok
    n_glob = global_pos.shape[0]
    seq_index = lax.axis_index("seq")
    group = seq_index // heads
    last = 1
    while 2 * last < n_groups:
        last *= 2
    ids = jnp.stack([seq_index % heads, group, lax.axis_index("head"), jnp.int32(last)])
    ids = ids.astype(jnp.int32)
    pos_col = global_pos.reshape(n_glob, 1)
    pos_row = global_pos.reshape(1, n_glob)

    def swap_in_group(pieces):
        moved = [
            lax.ppermute(piece, "seq", [(s, s ^ i) for s in range(n_seq)])
            for i, piece in enumerate(pieces)
            if i
        ]
        return [pieces[0]] + moved

    def from_first(x):
        d = 1
        while True:
            route = [
                (g * heads + j, (g + d) * heads + j)
                for g in range(d)
                for j in range(heads)
                if g + d < n_groups
            ]
            sent = lax.ppermute(x, "seq", route)
            if 2 * d >= n_groups:
                return x, sent
            x = jnp.where((group >= d) & (group < 2 * d), sent, x)
            d *= 2

    def to_next_group(x, step):
        route = [(s, s + step * heads) for s in range(n_seq) if 0 <= s + step * heads < n_seq]
        return lax.ppermute(x, "seq", route)

    def with_group(x, d):
        return lax.ppermute(x, "seq", [(s, s ^ (d * heads)) for s in range(n_seq)])

    kv_packed = local_call(
        "pack_kv",
        pack_kv_body,
        ids,
        (),
        [((2 * tok, HEAD_DIM), BF)] * heads,
        [pltpu.SemaphoreType.DMA((2 * heads,))],
        far=((in_hbm(keys), pltpu.HBM), (in_hbm(values), pltpu.HBM)),
        mib=PACK_MIB,
        out_space=pltpu.VMEM,
    )
    kv = swap_in_group(kv_packed)
    qo = swap_in_group(
        local_call(
            "pack_qo",
            pack_qo_body,
            ids,
            (queries, out_grad, out_weight),
            [((2 * tok + block_mask.size, HEAD_DIM), BF)] * heads,
            [pltpu.VMEM((tok, cols), BF)],
            far=((block_mask, pltpu.SMEM),),
            after=(kv_packed[0],),
        )
    )
    head_rows = ((total, HEAD_DIM), BF)
    head_sums = ((total, HEAD_DIM), F32)
    glob_sums = ((n_glob, HEAD_DIM), F32)
    k, v, key_bias, picked = local_call(
        "join_kv",
        join_kv_body,
        ids,
        (pos_col, pos_row, *kv),
        [
            head_rows,
            head_rows,
            ((tok, HEAD_DIM), F32),
            ((2 * n_glob, HEAD_DIM), BF),
        ],
    )
    kv_own, kv_sent = from_first(picked)
    kv_glob = jnp.where(group >= last, kv_sent, kv_own)
    kt, vt, rim_out = local_call(
        "turn",
        turn_body,
        ids,
        (k, v),
        [((HEAD_DIM, total), BF)] * 2 + [((2 * RIM, HEAD_DIM), BF)],
        after=(picked,),
    )
    rim_out, qo[2] = lax.optimization_barrier((rim_out, qo[2]))
    rim = to_next_group(rim_out, 1)
    q, d_attn, bias, qo_pick = local_call(
        "join_qo",
        join_qo_body,
        ids,
        (pos_col, pos_row, *qo),
        [
            head_rows,
            head_rows,
            ((heads * block_mask.size, HEAD_DIM), F32),
            ((2 * n_glob, HEAD_DIM), BF),
        ],
        after=(picked,),
    )
    qo_glob = from_first(qo_pick)
    n_steps = total // QROWS
    base = (q, k, vt, bias, key_bias)
    stat_rows = ((n_steps, QROWS), F32)
    forward_types = [
        ((n_steps * N_KEYS, QROWS), BF),
        ((n_steps * HEAD_DIM, QROWS), F32),
        stat_rows,
        stat_rows,
    ]

    def window(name, body, args, state, outs, scratch=(), after=()):
        at = 1 + len(args)
        return local_call(
            name,
            body,
            ids,
            tuple(args) + tuple(state),
            outs,
            scratch,
            after=after,
            aliases={at + i: i for i in range(len(state))},
            mib=20,
        )

    seen = window(
        "forward_inner",
        functools.partial(window_forward_body, range(2, n_steps), False),
        base,
        (),
        forward_types,
    )
    win_weights, *seen = window(
        "forward_rim",
        functools.partial(window_forward_body, range(0, 2), True),
        base + (rim,),
        seen,
        forward_types,
    )
    attn, glob_weights, d_win, d_glob, delta_win, delta_glob = local_call(
        "glob_forward",
        glob_forward_body,
        ids,
        (q, d_attn, kv_glob, *seen),
        [
            head_rows,
            ((n_steps * n_glob, QROWS), BF),
            head_rows,
            head_rows,
            stat_rows,
            stat_rows,
        ],
        mib=20,
    )
    backward = (q, d_win, kt, v, win_weights, delta_win)
    dq_rim, *state, rim_sum = window(
        "backward_rim",
        functools.partial(window_backward_body, range(0, 2), True),
        backward + (rim,),
        (),
        [((2 * HEAD_DIM, QROWS), F32), head_sums, head_sums, ((2 * RIM, HEAD_DIM), BF)],
        [pltpu.VMEM((RIM, HEAD_DIM), F32)] * 2,
    )
    rim_back = to_next_group(rim_sum, -1)
    packed_rows = ((HEAD_DIM + 16, n_glob), BF)
    mine = local_call(
        "row_forward",
        row_forward_body,
        ids,
        (*qo_glob, k, v, vt),
        [packed_rows],
        [pltpu.VMEM((total, n_glob), F32)],
        after=(rim_sum,),
    )[0]
    d = 1
    while 2 * d < n_groups:
        mine = local_call("merge", merge_body, ids, (mine, with_group(mine, d)), [packed_rows])[0]
        d *= 2
    other = with_group(mine, d)
    dq_part, dkg, dvg = local_call(
        "glob_backward",
        glob_backward_body,
        ids,
        (q, d_glob, kv_glob, glob_weights, delta_glob),
        [((n_steps * HEAD_DIM, QROWS), F32), glob_sums, glob_sums],
        after=(mine,),
    )
    rk, rv, sums = local_call(
        "row_backward",
        row_backward_body,
        ids,
        (*qo_glob, k, v, kt, mine, other, dkg, dvg),
        [head_sums, head_sums, ((3 * n_glob, HEAD_DIM), BF)],
    )
    attn_parts = swap_in_group(
        local_call(
            "pack_rows",
            pack_rows_body,
            ids,
            (pos_row, attn, mine, other),
            [((tok, HEAD_DIM), BF)] * heads,
            [pltpu.VMEM((total, HEAD_DIM), BF)],
            after=(sums,),
        )
    )
    dk, dv, dq = window(
        "backward_inner",
        functools.partial(window_backward_body, range(2, n_steps), False),
        backward + (dq_part, dq_rim),
        state,
        [head_sums, head_sums, head_rows],
        after=(attn_parts[0],),
    )

    def to_lower(x, d):
        route = [
            (g * heads + j, (g - d) * heads + j)
            for g in range(d, min(2 * d, n_groups))
            for j in range(heads)
        ]
        return lax.ppermute(x, "seq", route)

    d = n_groups // 2
    while d > 1:
        sums = (sums.astype(F32) + to_lower(sums, d).astype(F32)).astype(BF)
        d //= 2
    other_sums = to_lower(sums, 1)
    grads = swap_in_group(
        local_call(
            "pack_grads",
            pack_grads_body,
            ids,
            (pos_row, dq, dk, dv, rk, rv, rim_back, sums, other_sums),
            [((3 * tok, HEAD_DIM), BF)] * heads,
            [
                pltpu.VMEM((total, HEAD_DIM), BF),
                pltpu.VMEM((total, HEAD_DIM), F32),
                pltpu.VMEM((total, HEAD_DIM), F32),
            ],
        )
    )
    n_head = lax.axis_size("head")
    out_cols = out_weight.shape[1] // n_head
    keep, send = local_call(
        "project",
        project_body,
        ids,
        (out_weight, *attn_parts),
        [((2, tok, out_cols), BF)] * 2,
        [pltpu.VMEM((tok, cols), BF)],
        after=(grads[0],),
    )
    half = lax.ppermute(send, "head", [(h, h ^ 1) for h in range(n_head)])
    summed = keep.astype(F32) + half.astype(F32)
    far = lax.ppermute(summed[1].astype(BF), "head", [(h, h ^ 2) for h in range(n_head)])
    layer_out = (summed[0] + far.astype(F32)).astype(BF)
    grad_queries, grad_keys, grad_values = local_call(
        "join_grads", join_grads_body, ids, tuple(grads), [((tok, cols), BF)] * 3, us=JOIN_US
    )
    return (layer_out, grad_queries, grad_keys, grad_values)


def solution(mesh):
    return jax.shard_map(
        on_device,
        mesh=mesh,
        in_specs=(
            P("seq", "head"),
            P("seq", "head"),
            P("seq", "head"),
            P("head", None),
            P("seq", None),
            P(),
            P("seq", None),
        ),
        out_specs=(P("seq", "head"), P("seq", "head"), P("seq", "head"), P("seq", "head")),
        check_vma=False,
    )
```

```python
import functools
import math

import jax
import jax.numpy as jnp
from jax import lax
from jax.experimental import pallas as pl
from jax.experimental.pallas import tpu as pltpu
from jax.sharding import PartitionSpec as P

HEAD_DIM = 128
BLOCK = 128
WBLK = 4
RIM = (WBLK - 1) * BLOCK
QROWS = 2 * BLOCK
SCALE = 1.0 / math.sqrt(HEAD_DIM)
SCALE2 = SCALE * math.log2(math.e)
BF = jnp.bfloat16
F32 = jnp.float32
NEG = float("-inf")
FLOOR = -1e30
JOIN_US = 12.0
PACK_MIB = 14


def nn(a, b):
    return lax.dot_general(a, b, (((1,), (0,)), ((), ())), preferred_element_type=F32)


def nt(a, b):
    return lax.dot_general(a, b, (((1,), (1,)), ((), ())), preferred_element_type=F32)


def rows(slot, count):
    return pl.ds(pl.multiple_of(slot * count, count), count)


def local_call(name, body, ids, arrays, outs, scratch=(), after=(), aliases=None, far=(), mib=14, us=0.0, out_space=pltpu.VMEM):
    first = 1 + len(arrays) + len(far)

    def kernel(*refs):
        body(*refs[:first], *refs[first + len(after) :])

    return pl.pallas_call(
        kernel,
        name=name,
        out_shape=tuple(jax.ShapeDtypeStruct(s, t) for s, t in outs),
        in_specs=[pl.BlockSpec(memory_space=pltpu.SMEM)]
        + [pl.BlockSpec(memory_space=pltpu.VMEM)] * len(arrays)
        + [pl.BlockSpec(memory_space=space) for _, space in far]
        + [pl.BlockSpec(memory_space=pl.ANY)] * len(after),
        out_specs=tuple(pl.BlockSpec(memory_space=out_space) for _ in outs),
        scratch_shapes=list(scratch),
        compiler_params=pltpu.CompilerParams(vmem_limit_bytes=mib * 2**20),
        input_output_aliases=aliases or {},
        cost_estimate=pl.CostEstimate(
            flops=1000 + int(us * 1.15e9), bytes_accessed=1000, transcendentals=0
        ),
    )(ids, *arrays, *[array for array, _ in far], *after)


def in_hbm(x):
    return pltpu.with_memory_space_constraint(x, pltpu.HBM)


def pack_kv_body(ids, k, v, *refs):
    outs, sems = refs[:-1], refs[-1]
    tok = k.shape[0]
    copies = []
    for i, out in enumerate(outs):
        col = rows(ids[0] ^ i, HEAD_DIM)
        copies += [
            pltpu.make_async_copy(k.at[:, col], out.at[0:tok, :], sems.at[2 * i]),
            pltpu.make_async_copy(v.at[:, col], out.at[tok:, :], sems.at[2 * i + 1]),
        ]
    for copy in copies:
        copy.start()
    for copy in copies:
        copy.wait()


def pack_qo_body(ids, q, out_grad, out_weight, block_mask, *refs):
    outs, d_attn = refs[:-1], refs[-1]
    tok = q.shape[0]
    entries = outs[0].shape[0] - 2 * tok
    at = lax.broadcasted_iota(jnp.int32, (entries, HEAD_DIM), 0)
    mask = jnp.zeros((entries, HEAD_DIM), jnp.int32)
    for e in range(entries):
        mask = jnp.where(at == e, block_mask[e // WBLK, e % WBLK], mask)
    mask = mask.astype(F32).astype(BF)
    d_attn[...] = nt(out_grad[...], out_weight[...]).astype(BF)
    for i, out in enumerate(outs):
        col = rows(ids[0] ^ i, HEAD_DIM)
        out[0:tok, :] = q[:, col]
        out[tok : 2 * tok, :] = d_attn[:, col]
        out[2 * tok :, :] = mask


def pick_rows(pos_col, tok):
    hits = pos_col == lax.broadcasted_iota(jnp.int32, (pos_col.shape[0], tok), 1)
    return hits.astype(BF)


def place_rows(pos_row, tok):
    return lax.broadcasted_iota(jnp.int32, (tok, pos_row.shape[1]), 0) == pos_row


def row_column(pos_row, tok):
    hit = place_rows(pos_row, tok).astype(F32)
    return jnp.max(hit, axis=1, keepdims=True) > 0.5


def join_kv_body(ids, pos_col, pos_row, *refs):
    pieces, (k, v, key_bias, picked) = refs[:-4], refs[-4:]
    tok = k.shape[0] // len(pieces)
    for i, piece in enumerate(pieces):
        slot = ids[0] ^ i
        k[rows(slot, tok), :] = piece[0:tok, :]
        v[rows(slot, tok), :] = piece[tok:, :]
    picks = pick_rows(pos_col[...], tok)
    n = pos_col.shape[0]
    picked[0:n, :] = nn(picks, k[0:tok, :]).astype(BF)
    picked[n:, :] = nn(picks, v[0:tok, :]).astype(BF)
    hidden = jnp.logical_and(row_column(pos_row[...], tok), ids[1] == 0)
    key_bias[...] = jnp.where(hidden, NEG, jnp.zeros(key_bias.shape, F32))


def turn_body(ids, k, v, kt, vt, rim):
    kt[...] = k[...].T
    vt[...] = v[...].T
    rim[0:RIM, :] = k[k.shape[0] - RIM :, :]
    rim[RIM:, :] = v[k.shape[0] - RIM :, :]


def join_qo_body(ids, pos_col, pos_row, *refs):
    pieces, (q, d_attn, bias, picked) = refs[:-4], refs[-4:]
    tok = q.shape[0] // len(pieces)
    n_rows = bias.shape[0] // len(pieces)
    n = pos_col.shape[0]
    for i, piece in enumerate(pieces):
        slot = ids[0] ^ i
        q[rows(slot, tok), :] = piece[0:tok, :]
        d_attn[rows(slot, tok), :] = piece[tok : 2 * tok, :]
        open_ = piece[2 * tok :, :].astype(F32)
        entry = lax.broadcasted_iota(jnp.int32, open_.shape, 0) + slot * n_rows
        inside = (ids[1] > 0) | (entry // WBLK >= entry % WBLK)
        bias[rows(slot, n_rows), :] = jnp.where((open_ > 0.5) & inside, 0.0, NEG)

    @pl.when(ids[1] == 0)
    def _():
        picks = pick_rows(pos_col[...], tok)
        picked[0:n, :] = nn(picks, q[0:tok, :]).astype(BF)
        picked[n:, :] = nn(picks, d_attn[0:tok, :]).astype(BF)
        is_row = row_column(pos_row[...], tok)
        kept = jnp.where(is_row, 0.0, d_attn[0:tok, :].astype(F32))
        d_attn[0:tok, :] = kept.astype(BF)

    @pl.when(ids[1] > 0)
    def _():
        picked[...] = jnp.zeros_like(picked)


def row_forward_body(ids, own, sent, k, v, vt, mine, scores):
    picked = ours(ids, own, sent)
    n = picked.shape[0] // 2
    step = 512
    query, d_out = picked[0:n, :], picked[n:, :]
    peak = None
    for c in range(0, k.shape[0], step):
        s = nt(k[c : c + step, :], query) * SCALE2
        scores[c : c + step, :] = s
        top = jnp.max(s, axis=0, keepdims=True)
        peak = top if peak is None else jnp.maximum(peak, top)
    mass = jnp.zeros((1, n), F32)
    dot = jnp.zeros((1, n), F32)
    numer = jnp.zeros((HEAD_DIM, n), F32)
    for c in range(0, k.shape[0], step):
        e = jnp.exp2(scores[c : c + step, :] - peak)
        vals = v[c : c + step, :]
        mass = mass + jnp.sum(e, axis=0, keepdims=True)
        dot = dot + jnp.sum(e * nt(vals, d_out), axis=0, keepdims=True)
        numer = numer + nn(vt[:, c : c + step], e.astype(BF))
    mine[0:HEAD_DIM, :] = (numer / mass).astype(BF)
    mine[HEAD_DIM:, :] = in_thirds((peak, mass, dot))


def in_thirds(values):
    parts = []
    for value in values:
        for _ in range(3):
            part = value.astype(BF).astype(F32)
            parts.append(part)
            value = value - part
    empty = jnp.zeros((16 - len(parts), parts[0].shape[1]), F32)
    return jnp.concatenate(parts + [empty], axis=0).astype(BF)


def merged(mine, other):
    thirds = [ref[HEAD_DIM:, :].astype(F32) for ref in (mine, other)]
    (pa, ma, da), (pb, mb, db) = [
        [t[3 * i : 3 * i + 1] + t[3 * i + 1 : 3 * i + 2] + t[3 * i + 2 : 3 * i + 3] for i in range(3)]
        for t in thirds
    ]
    peak = jnp.maximum(pa, pb)
    wa, wb = jnp.exp2(pa - peak), jnp.exp2(pb - peak)
    mass = ma * wa + mb * wb
    return peak, mass, da * wa + db * wb, ma * wa / mass, mb * wb / mass


def merged_attn(mine, other, wa, wb):
    both = mine[0:HEAD_DIM, :].astype(F32) * wa + other[0:HEAD_DIM, :].astype(F32) * wb
    return both.astype(BF)


def merge_body(ids, mine, other, out):
    peak, mass, dot, wa, wb = merged(mine, other)
    out[0:HEAD_DIM, :] = merged_attn(mine, other, wa, wb)
    out[HEAD_DIM:, :] = in_thirds((peak, mass, dot))


N_KEYS = RIM + QROWS


def window_span(sb):
    first = sb * QROWS - RIM
    cut = max(0, -first)
    return first, cut, slice(first + cut, (sb + 1) * QROWS)


def window_rows(sb, own, rim):
    _, cut, inner = window_span(sb)
    if not cut:
        return own[inner, :]
    return jnp.concatenate([rim[RIM - cut : RIM, :], own[inner, :]], axis=0)


def window_cols(sb, own_t, rim):
    _, cut, inner = window_span(sb)
    if not cut:
        return own_t[:, inner]
    return jnp.concatenate([rim[RIM - cut : RIM, :].T, own_t[:, inner]], axis=1)


def window_forward_body(steps, with_rim, ids, *refs):
    q, k, vt, bias, key_bias = refs[:5]
    k_rim, v_rim = (refs[5].at[0:RIM], refs[5].at[RIM:]) if with_rim else (None, None)
    weights, out_t, peaks, masses = refs[-4:]
    key_in = lax.broadcasted_iota(jnp.int32, (BLOCK, QROWS), 0)
    query_in = lax.broadcasted_iota(jnp.int32, (BLOCK, QROWS), 1)
    shut = jnp.full((1, BLOCK), NEG, F32)
    for sb in steps:
        here = slice(sb * QROWS, (sb + 1) * QROWS)
        first = window_span(sb)[0]
        kw, vwt = window_rows(sb, k, k_rim), window_cols(sb, vt, v_rim)
        raw = nt(kw, q[here, :])
        parts = []
        for kb in range(N_KEYS // BLOCK):
            halves = []
            for half in range(QROWS // BLOCK):
                r = half + WBLK - 1 - kb
                at = (sb * (QROWS // BLOCK) + half) * WBLK + r
                halves.append(bias[at : at + 1, :] if 0 <= r < WBLK else shut)
            part = raw[kb * BLOCK : (kb + 1) * BLOCK, :] * SCALE2 + jnp.concatenate(halves, axis=1)
            at = first + kb * BLOCK
            if 0 <= at < key_bias.shape[0]:
                col = key_bias[at : at + BLOCK, :]
                part = part + jnp.concatenate([col] * (QROWS // BLOCK), axis=1)
            own = kb - (WBLK - 1)
            if own >= 0:
                part = jnp.where(query_in - key_in >= own * BLOCK, part, NEG)
            parts.append(part)
        peak = jnp.full((1, QROWS), FLOOR, F32)
        for part in parts:
            peak = jnp.maximum(peak, part.max(axis=0, keepdims=True))
        grown = [jnp.exp2(part - peak) for part in parts]
        masses[sb : sb + 1, :] = sum(e.sum(axis=0, keepdims=True) for e in grown)
        peaks[sb : sb + 1, :] = peak
        ww = jnp.concatenate([e.astype(BF) for e in grown], axis=0)
        weights[sb * N_KEYS : (sb + 1) * N_KEYS, :] = ww
        out_t[sb * HEAD_DIM : (sb + 1) * HEAD_DIM, :] = nn(vwt, ww)


def ours(ids, mine, sent):
    return jnp.where(ids[1] < ids[3], mine[...], sent[...])


def glob_forward_body(ids, q, d_out, picked, out_t, peaks, masses, *refs):
    attn, weights, d_win, d_glob, delta_win, delta_glob = refs
    n = picked.shape[0] // 2
    kg, vgt = picked[0:n, :], picked[n:, :].T
    for sb in range(peaks.shape[0]):
        here = slice(sb * QROWS, (sb + 1) * QROWS)
        row = slice(sb, sb + 1)
        score = nt(kg, q[here, :]) * SCALE2
        peak = jnp.maximum(peaks[row, :], score.max(axis=0, keepdims=True))
        grown = jnp.exp2(score - peak)
        part = jnp.exp2(peaks[row, :] - peak)
        inv = 1.0 / (masses[row, :] * part + grown.sum(axis=0, keepdims=True))
        part = part * inv
        wg = grown.astype(BF)
        weights[sb * n : (sb + 1) * n, :] = wg
        both = out_t[sb * HEAD_DIM : (sb + 1) * HEAD_DIM, :] * part + nn(vgt, wg) * inv
        attn[here, :] = both.T.astype(BF)
        d_t = d_out[here, :].astype(F32).T
        delta = jnp.sum(both.astype(BF).astype(F32) * d_t, axis=0, keepdims=True)
        d_win[here, :] = (d_t * part).T.astype(BF)
        d_glob[here, :] = (d_t * inv).T.astype(BF)
        delta_win[row, :] = delta * part
        delta_glob[row, :] = delta * inv


def glob_backward_body(ids, q, d_out, picked, weights, delta, dq_part, dk_glob, dv_glob):
    n = picked.shape[0] // 2
    n_steps = delta.shape[0]
    kt, vg = picked[0:n, :].T, picked[n:, :]
    wide = 2
    dkg = jnp.zeros(dk_glob.shape, F32)
    dvg = jnp.zeros(dv_glob.shape, F32)
    for c in range(0, n_steps, wide):
        here = slice(c * QROWS, (c + wide) * QROWS)
        qb, dob = q[here, :], d_out[here, :]
        wg = jnp.concatenate(
            [weights[sb * n : (sb + 1) * n, :] for sb in range(c, c + wide)], axis=1
        )
        off = jnp.concatenate([delta[sb : sb + 1, :] for sb in range(c, c + wide)], axis=1)
        dg = (wg.astype(F32) * (nt(vg, dob) - off)).astype(BF)
        dq_t = nn(kt, dg)
        for i in range(wide):
            dq_part[(c + i) * HEAD_DIM : (c + i + 1) * HEAD_DIM, :] = dq_t[:, i * QROWS : (i + 1) * QROWS]
        dkg = dkg + nn(dg, qb)
        dvg = dvg + nn(wg, dob)
    dk_glob[...] = dkg
    dv_glob[...] = dvg


def window_backward_body(steps, with_rim, ids, *refs):
    q, d_out, kt, v, weights, delta = refs[:6]
    k_rim, v_rim = (refs[6].at[0:RIM], refs[6].at[RIM:]) if with_rim else (None, None)
    if with_rim:
        dq_rim, dk, dv, rim_back, dk_rim, dv_rim = refs[-6:]
        for ref in (dk, dv, dk_rim, dv_rim):
            ref[...] = jnp.zeros_like(ref)
    else:
        dq_part, dq_rim = refs[6:8]
        dk, dv, dq = refs[-3:]
        for sb in range(dq_rim.shape[0] // HEAD_DIM):
            here = slice(sb * HEAD_DIM, (sb + 1) * HEAD_DIM)
            dq_t = dq_rim[here, :] + dq_part[here, :]
            dq[sb * QROWS : (sb + 1) * QROWS, :] = (dq_t.T * SCALE).astype(BF)
    for sb in steps:
        here = slice(sb * QROWS, (sb + 1) * QROWS)
        _, cut, inner = window_span(sb)
        kwt, vw = window_cols(sb, kt, k_rim), window_rows(sb, v, v_rim)
        qb, dob = q[here, :], d_out[here, :]
        ww = weights[sb * N_KEYS : (sb + 1) * N_KEYS, :]
        dw = (ww.astype(F32) * (nt(vw, dob) - delta[sb : sb + 1, :])).astype(BF)
        part = slice(sb * HEAD_DIM, (sb + 1) * HEAD_DIM)
        if with_rim:
            dq_rim[part, :] = nn(kwt, dw)
        else:
            dq_t = nn(kwt, dw) + dq_part[part, :]
            dq[here, :] = (dq_t.T * SCALE).astype(BF)
        dkw, dvw = nn(dw, qb), nn(ww, dob)
        if cut:
            dk_rim[RIM - cut :, :] += dkw[0:cut, :]
            dv_rim[RIM - cut :, :] += dvw[0:cut, :]
        dk[inner, :] += dkw[cut:, :]
        dv[inner, :] += dvw[cut:, :]
    if with_rim:
        rim_back[0:RIM, :] = dk_rim[...].astype(BF)
        rim_back[RIM:, :] = dv_rim[...].astype(BF)


def row_backward_body(ids, own, sent, k, v, kt, mine, other, dkg, dvg, dk, dv, sums):
    picked = ours(ids, own, sent)
    n = picked.shape[0] // 2
    step = 512
    query, d_out = picked[0:n, :], picked[n:, :]
    peak, mass, dot, _, _ = merged(mine, other)
    lse = peak + jnp.log2(mass)
    delta = dot / mass
    dq_t = jnp.zeros((HEAD_DIM, n), F32)
    for c in range(0, k.shape[0], step):
        keys, vals = k[c : c + step, :], v[c : c + step, :]
        prob = jnp.exp2(nt(keys, query) * SCALE2 - lse)
        ds = (prob * (nt(vals, d_out) - delta)).astype(BF)
        dk[c : c + step, :] = nn(ds, query)
        dv[c : c + step, :] = nn(prob.astype(BF), d_out)
        dq_t = dq_t + nn(kt[:, c : c + step], ds)
    sums[0:n, :] = (dq_t.T * SCALE).astype(BF)
    sums[n : 2 * n, :] = dkg[...].astype(BF)
    sums[2 * n :, :] = dvg[...].astype(BF)


def pack_rows_body(ids, pos_row, attn, mine, other, *refs):
    outs, attn_f = refs[:-1], refs[-1]
    tok = attn.shape[0] // len(outs)
    attn_f[...] = attn[...]

    @pl.when(ids[1] == 0)
    def _():
        _, _, _, wa, wb = merged(mine, other)
        both_t = merged_attn(mine, other, wa, wb)
        hit = place_rows(pos_row[...], tok)
        is_row = jnp.max(hit.astype(F32), axis=1, keepdims=True) > 0.5
        placed = nt(hit.astype(BF), both_t)
        attn_f[0:tok, :] = jnp.where(is_row, placed, attn[0:tok, :].astype(F32)).astype(BF)

    for i, out in enumerate(outs):
        out[...] = attn_f[rows(ids[0] ^ i, tok), :]


def project_body(ids, w, *refs):
    pieces, (keep, send, attn) = refs[:-3], refs[-3:]
    for i, piece in enumerate(pieces):
        attn[:, rows(ids[0] ^ i, HEAD_DIM)] = piece[...]
    cols = keep.shape[2]
    a = attn[...]
    me = ids[2]
    for i, group in enumerate((me, me ^ 2)):
        keep[i] = nn(a, w[:, rows(group, cols)]).astype(BF)
    for i, group in enumerate((me ^ 1, me ^ 3)):
        send[i] = nn(a, w[:, rows(group, cols)]).astype(BF)


def pack_grads_body(ids, pos_row, dq, dk, dv, rk, rv, rim_back, sums, other, *refs):
    outs, (dqf, dkf, dvf) = refs[:-3], refs[-3:]
    total = dk.shape[0]
    tok = total // len(outs)
    n = sums.shape[0] // 3
    dqf[...] = dq[...]
    dkf[...] = dk[...] + rk[...]
    dvf[...] = dv[...] + rv[...]
    dkf[total - RIM :, :] += rim_back[0:RIM, :].astype(F32)
    dvf[total - RIM :, :] += rim_back[RIM:, :].astype(F32)

    @pl.when(ids[1] == 0)
    def _():
        both = (sums[...].astype(F32) + other[...].astype(F32)).astype(BF)
        hit = place_rows(pos_row[...], tok).astype(BF)
        dqf[0:tok, :] = (dqf[0:tok, :].astype(F32) + nn(hit, both[0:n, :])).astype(BF)
        dkf[0:tok, :] += nn(hit, both[n : 2 * n, :])
        dvf[0:tok, :] += nn(hit, both[2 * n :, :])

    for i, out in enumerate(outs):
        here = rows(ids[0] ^ i, tok)
        out[0:tok, :] = dqf[here, :]
        out[tok : 2 * tok, :] = (dkf[here, :] * SCALE).astype(BF)
        out[2 * tok :, :] = dvf[here, :].astype(BF)


def join_grads_body(ids, *refs):
    pieces, outs = refs[:-3], refs[-3:]
    tok = outs[0].shape[0]
    for i, piece in enumerate(pieces):
        col = rows(ids[0] ^ i, HEAD_DIM)
        for at, out in enumerate(outs):
            out[:, col] = piece[at * tok : (at + 1) * tok, :]


def on_device(queries, keys, values, out_weight, out_grad, global_pos, block_mask):
    tok, cols = queries.shape
    heads = cols // HEAD_DIM
    n_seq = lax.axis_size("seq")
    n_groups = n_seq // heads
    total = heads * tok
    n_glob = global_pos.shape[0]
    seq_index = lax.axis_index("seq")
    group = seq_index // heads
    last = 1
    while 2 * last < n_groups:
        last *= 2
    ids = jnp.stack([seq_index % heads, group, lax.axis_index("head"), jnp.int32(last)])
    ids = ids.astype(jnp.int32)
    pos_col = global_pos.reshape(n_glob, 1)
    pos_row = global_pos.reshape(1, n_glob)

    def swap_in_group(pieces):
        moved = [
            lax.ppermute(piece, "seq", [(s, s ^ i) for s in range(n_seq)])
            for i, piece in enumerate(pieces)
            if i
        ]
        return [pieces[0]] + moved

    def from_first(x):
        d = 1
        while True:
            route = [
                (g * heads + j, (g + d) * heads + j)
                for g in range(d)
                for j in range(heads)
                if g + d < n_groups
            ]
            sent = lax.ppermute(x, "seq", route)
            if 2 * d >= n_groups:
                return x, sent
            x = jnp.where((group >= d) & (group < 2 * d), sent, x)
            d *= 2

    def to_next_group(x, step):
        route = [(s, s + step * heads) for s in range(n_seq) if 0 <= s + step * heads < n_seq]
        return lax.ppermute(x, "seq", route)

    def with_group(x, d):
        return lax.ppermute(x, "seq", [(s, s ^ (d * heads)) for s in range(n_seq)])

    kv_packed = local_call(
        "pack_kv",
        pack_kv_body,
        ids,
        (),
        [((2 * tok, HEAD_DIM), BF)] * heads,
        [pltpu.SemaphoreType.DMA((2 * heads,))],
        far=((in_hbm(keys), pltpu.HBM), (in_hbm(values), pltpu.HBM)),
        mib=PACK_MIB,
        out_space=pltpu.VMEM,
    )
    kv = swap_in_group(kv_packed)
    qo = swap_in_group(
        local_call(
            "pack_qo",
            pack_qo_body,
            ids,
            (in_hbm(queries), in_hbm(out_grad), in_hbm(out_weight)),
            [((2 * tok + block_mask.size, HEAD_DIM), BF)] * heads,
            [pltpu.VMEM((tok, cols), BF)],
            far=((block_mask, pltpu.SMEM),),
            after=(kv_packed[0],),
        )
    )
    head_rows = ((total, HEAD_DIM), BF)
    head_sums = ((total, HEAD_DIM), F32)
    glob_sums = ((n_glob, HEAD_DIM), F32)
    k, v, key_bias, picked = local_call(
        "join_kv",
        join_kv_body,
        ids,
        (pos_col, pos_row, *kv),
        [
            head_rows,
            head_rows,
            ((tok, HEAD_DIM), F32),
            ((2 * n_glob, HEAD_DIM), BF),
        ],
    )
    kv_own, kv_sent = from_first(picked)
    kv_glob = jnp.where(group >= last, kv_sent, kv_own)
    kt, vt, rim_out = local_call(
        "turn",
        turn_body,
        ids,
        (k, v),
        [((HEAD_DIM, total), BF)] * 2 + [((2 * RIM, HEAD_DIM), BF)],
        after=(picked,),
    )
    rim_out, qo[2] = lax.optimization_barrier((rim_out, qo[2]))
    rim = to_next_group(rim_out, 1)
    q, d_attn, bias, qo_pick = local_call(
        "join_qo",
        join_qo_body,
        ids,
        (pos_col, pos_row, *qo),
        [
            head_rows,
            head_rows,
            ((heads * block_mask.size, HEAD_DIM), F32),
            ((2 * n_glob, HEAD_DIM), BF),
        ],
        after=(picked,),
    )
    qo_glob = from_first(qo_pick)
    n_steps = total // QROWS
    base = (q, k, vt, bias, key_bias)
    stat_rows = ((n_steps, QROWS), F32)
    forward_types = [
        ((n_steps * N_KEYS, QROWS), BF),
        ((n_steps * HEAD_DIM, QROWS), F32),
        stat_rows,
        stat_rows,
    ]

    def window(name, body, args, state, outs, scratch=(), after=()):
        at = 1 + len(args)
        return local_call(
            name,
            body,
            ids,
            tuple(args) + tuple(state),
            outs,
            scratch,
            after=after,
            aliases={at + i: i for i in range(len(state))},
            mib=20,
        )

    seen = window(
        "forward_inner",
        functools.partial(window_forward_body, range(2, n_steps), False),
        base,
        (),
        forward_types,
    )
    win_weights, *seen = window(
        "forward_rim",
        functools.partial(window_forward_body, range(0, 2), True),
        base + (rim,),
        seen,
        forward_types,
    )
    attn, glob_weights, d_win, d_glob, delta_win, delta_glob = local_call(
        "glob_forward",
        glob_forward_body,
        ids,
        (q, d_attn, kv_glob, *seen),
        [
            head_rows,
            ((n_steps * n_glob, QROWS), BF),
            head_rows,
            head_rows,
            stat_rows,
            stat_rows,
        ],
        mib=20,
    )
    backward = (q, d_win, kt, v, win_weights, delta_win)
    dq_rim, *state, rim_sum = window(
        "backward_rim",
        functools.partial(window_backward_body, range(0, 2), True),
        backward + (rim,),
        (),
        [((2 * HEAD_DIM, QROWS), F32), head_sums, head_sums, ((2 * RIM, HEAD_DIM), BF)],
        [pltpu.VMEM((RIM, HEAD_DIM), F32)] * 2,
    )
    rim_back = to_next_group(rim_sum, -1)
    packed_rows = ((HEAD_DIM + 16, n_glob), BF)
    mine = local_call(
        "row_forward",
        row_forward_body,
        ids,
        (*qo_glob, k, v, vt),
        [packed_rows],
        [pltpu.VMEM((total, n_glob), F32)],
        after=(rim_sum,),
    )[0]
    d = 1
    while 2 * d < n_groups:
        mine = local_call("merge", merge_body, ids, (mine, with_group(mine, d)), [packed_rows])[0]
        d *= 2
    other = with_group(mine, d)
    dq_part, dkg, dvg = local_call(
        "glob_backward",
        glob_backward_body,
        ids,
        (q, d_glob, kv_glob, glob_weights, delta_glob),
        [((n_steps * HEAD_DIM, QROWS), F32), glob_sums, glob_sums],
        after=(mine,),
    )
    rk, rv, sums = local_call(
        "row_backward",
        row_backward_body,
        ids,
        (*qo_glob, k, v, kt, mine, other, dkg, dvg),
        [head_sums, head_sums, ((3 * n_glob, HEAD_DIM), BF)],
    )
    attn_parts = swap_in_group(
        local_call(
            "pack_rows",
            pack_rows_body,
            ids,
            (pos_row, attn, mine, other),
            [((tok, HEAD_DIM), BF)] * heads,
            [pltpu.VMEM((total, HEAD_DIM), BF)],
            after=(sums,),
        )
    )
    dk, dv, dq = window(
        "backward_inner",
        functools.partial(window_backward_body, range(2, n_steps), False),
        backward + (dq_part, dq_rim),
        state,
        [head_sums, head_sums, head_rows],
        after=(attn_parts[0],),
    )

    def to_lower(x, d):
        route = [
            (g * heads + j, (g - d) * heads + j)
            for g in range(d, min(2 * d, n_groups))
            for j in range(heads)
        ]
        return lax.ppermute(x, "seq", route)

    d = n_groups // 2
    while d > 1:
        sums = (sums.astype(F32) + to_lower(sums, d).astype(F32)).astype(BF)
        d //= 2
    other_sums = to_lower(sums, 1)
    grads = swap_in_group(
        local_call(
            "pack_grads",
            pack_grads_body,
            ids,
            (pos_row, dq, dk, dv, rk, rv, rim_back, sums, other_sums),
            [((3 * tok, HEAD_DIM), BF)] * heads,
            [
                pltpu.VMEM((total, HEAD_DIM), BF),
                pltpu.VMEM((total, HEAD_DIM), F32),
                pltpu.VMEM((total, HEAD_DIM), F32),
            ],
        )
    )
    n_head = lax.axis_size("head")
    out_cols = out_weight.shape[1] // n_head
    keep, send = local_call(
        "project",
        project_body,
        ids,
        (out_weight, *attn_parts),
        [((2, tok, out_cols), BF)] * 2,
        [pltpu.VMEM((tok, cols), BF)],
        after=(grads[0],),
    )
    half = lax.ppermute(send, "head", [(h, h ^ 1) for h in range(n_head)])
    summed = keep.astype(F32) + half.astype(F32)
    far = lax.ppermute(summed[1].astype(BF), "head", [(h, h ^ 2) for h in range(n_head)])
    layer_out = (summed[0] + far.astype(F32)).astype(BF)
    grad_queries, grad_keys, grad_values = local_call(
        "join_grads", join_grads_body, ids, tuple(grads), [((tok, cols), BF)] * 3, us=JOIN_US
    )
    return (layer_out, grad_queries, grad_keys, grad_values)


def solution(mesh):
    return jax.shard_map(
        on_device,
        mesh=mesh,
        in_specs=(
            P("seq", "head"),
            P("seq", "head"),
            P("seq", "head"),
            P("head", None),
            P("seq", None),
            P(),
            P("seq", None),
        ),
        out_specs=(P("seq", "head"), P("seq", "head"), P("seq", "head"), P("seq", "head")),
        check_vma=False,
    )
```
